512 devices in a mesh: blk: 32 (over z, core), line: 16 (over y, x).
Axes of the slice: x: 4, y: 4, z: 16, core: 2. Of those that a mesh axis runs over, the one named last changes fastest.
Arguments:
- right_side: bfloat16 [384, 2048, 128], P('blk', 'line'), may hold values from -6 to 6
- diagonal_inverse: bfloat16 [384, 128, 128], P('blk', 'line')
- lower_blocks: bfloat16 [384, 3, 128, 128], P('blk', None, 'line'), may hold values from -0.25 to 0.25
- upper_blocks: bfloat16 [384, 3, 128, 128], P('blk', None, 'line'), may hold values from -0.25 to 0.25
- row_level: int32 [384], P('blk'), may hold values from 0 to 5, as said below
- lower_links: int32 [384, 3], P('blk'), may hold values from -1 to 383, as said below
- upper_links: int32 [384, 3], P('blk'), may hold values from -1 to 383, as said below
Outputs:
- smoothed: bfloat16 [384, 2048, 128], P('blk', 'line')
The draws below stay inside these ranges and needn't reach their ends.
Inputs may be any that keep to these rules, and one draw needn't show every extreme that they name: `row_level`: the 12 block rows of every blk index hold every level, at most 3 of them at one level, and some level holds exactly 3 of them on every index. `lower_links`: -1 marks an empty slot. Rows of level 0 have only empty slots, all other rows none. Every other entry names a block row of lower level held by the same blk index or by one next to it (never across the ends of the axis); a row held by a neighbouring index is always the lowest-numbered row of its level there. `upper_links`: -1 marks an empty slot. Rows of level 5 have only empty slots, all other rows none. Every other entry names a block row of higher level held by the same blk index or by one next to it (never across the ends of the axis); a row held by a neighbouring index is always the lowest-numbered row of its level there.
All inputs are finite; a program needn't handle non-finite values.
Results may differ from the reference program's by a relative error of at most 0.0085.
Values may be sent and summed in bfloat16 or wider, within the bound.
No kernel may reach another device: no remote copies, remote signals or barrier semaphores. Data moves between devices by JAX's collectives and lax.ppermute only.
A program may use at most 64 MiB of HBM per device.

```python
import jax
import jax.numpy as jnp
import numpy as np
from jax import lax

VARS = 128
LINKS = 3
LEVELS = 6
ROWS_DEV = 12
BLOCK_ROWS = 384
LINES = 2048


PATTERNS = np.array([[3, 3, 2, 2, 1, 1], [3, 2, 2, 2, 2, 1], [3, 3, 3, 1, 1, 1]], dtype=np.int32)


def block_levels(key):
    devices = BLOCK_ROWS // ROWS_DEV
    key_list = jax.random.split(jax.random.fold_in(key, 11), devices)

    def one_device(dev_key):
        key_pick, key_count, key_order = jax.random.split(dev_key, 3)
        pattern = jax.random.randint(key_pick, (), 0, 3)
        counts = jnp.asarray(PATTERNS, jnp.int32)[pattern]
        counts = jax.random.permutation(key_count, counts)
        bounds = jnp.cumsum(counts)
        places = jnp.arange(ROWS_DEV, dtype=jnp.int32)
        sorted_levels = jnp.sum((bounds[None, :] <= places[:, None]).astype(jnp.int32), axis=1)
        shuffle = jax.random.permutation(key_order, ROWS_DEV)
        return sorted_levels[shuffle]
    return jax.vmap(one_device)(key_list)


def neighbour_lists(key, upward):
    level_table = block_levels(key)
    devices = level_table.shape[0]
    stream = 23 if upward else 37
    key_side, key_level, key_rank = jax.random.split(jax.random.fold_in(key, stream), 3)
    grid_shape = (devices, ROWS_DEV, LINKS)
    own_device = jnp.broadcast_to(jnp.arange(devices, dtype=jnp.int32)[:, None, None], grid_shape)
    own_level = jnp.broadcast_to(level_table[:, :, None], grid_shape)
    offset = jax.random.randint(key_side, grid_shape, -1, 2)
    holder = own_device + offset
    holder = jnp.where((holder < 0) | (holder >= devices), own_device, holder)
    offset = holder - own_device
    if upward:
        spread = LEVELS - 1 - own_level
        drawn = jax.random.randint(key_level, grid_shape, 0, jnp.maximum(spread, 1))
        target = own_level + 1 + drawn
        vacant = own_level == LEVELS - 1
    else:
        spread = own_level
        target = jax.random.randint(key_level, grid_shape, 0, jnp.maximum(spread, 1))
        vacant = own_level == 0
    target = jnp.where(vacant, 0, target)
    holder_levels = level_table[holder]
    matched = holder_levels == target[..., None]
    counts = jnp.sum(matched.astype(jnp.int32), axis=-1)
    ranking = jax.random.randint(key_rank, grid_shape, 0, jnp.maximum(counts, 1))
    ranking = jnp.where(offset == 0, ranking, 0)
    running = jnp.cumsum(matched.astype(jnp.int32), axis=-1) - 1
    chosen = jnp.argmax(matched & (running == ranking[..., None]), axis=-1).astype(jnp.int32)
    position = holder * ROWS_DEV + chosen
    return jnp.where(vacant, -1, position).reshape(devices * ROWS_DEV, LINKS).astype(jnp.int32)


def draw_row_level(key, part):
    return block_levels(key).reshape(-1).astype(jnp.int32)


def draw_lower_links(key, part):
    return neighbour_lists(key, False)


def draw_upper_links(key, part):
    return neighbour_lists(key, True)


def draw_diagonal_inverse(key, part):
    sub_key = jax.random.fold_in(key, 51)
    random_part = jax.random.normal(sub_key, (BLOCK_ROWS, VARS, VARS), jnp.float32)
    identity = jnp.eye(VARS, dtype=jnp.float32)
    return (0.5 * identity[None] + 0.5 * VARS ** (-0.5) * random_part).astype(jnp.bfloat16)


def level_of(rng, dims, pieces, least, high):
    factor_of = 1.0
    for axis_at, shards_of in pieces:
        heights = jax.random.uniform(jax.random.fold_in(jax.random.fold_in(rng, 6), axis_at), (shards_of,), jnp.float32, least / len(pieces), high / len(pieces))
        factor_of = factor_of * jnp.repeat(jnp.exp(heights), dims[axis_at] // shards_of).reshape((-1,) + (1,) * (len(dims) - 1 - axis_at))
    return factor_of


def noise(stream_key, shape, scale, limit, shards=(), kind=jnp.bfloat16):
    level = level_of(stream_key, shape, shards, -0.22, 0.18) if shards else 1.0
    values = jax.random.normal(stream_key, shape, jnp.float32) * scale * level
    return jnp.minimum(jnp.maximum(values, -limit), limit).astype(kind)


def setup_inputs(seed: int = 0) -> dict:
    arg_keys = jax.random.split(jax.random.key(seed), 8)
    right_side = noise(arg_keys[0], (BLOCK_ROWS, LINES, VARS), 1.0, 6.0, ((0, 32), (1, 16)))
    diagonal_inverse = draw_diagonal_inverse(jax.random.fold_in(arg_keys[7], 71), 0)
    lower_blocks = noise(arg_keys[2], (BLOCK_ROWS, LINKS, VARS, VARS), (4 * VARS) ** -0.5, 0.25, ((0, 32), (2, 16)))
    upper_blocks = noise(arg_keys[3], (BLOCK_ROWS, LINKS, VARS, VARS), (4 * VARS) ** -0.5, 0.25, ((0, 32), (2, 16)))
    row_level = draw_row_level(jax.random.fold_in(arg_keys[7], 71), 0)
    lower_links = draw_lower_links(jax.random.fold_in(arg_keys[7], 71), 0)
    upper_links = draw_upper_links(jax.random.fold_in(arg_keys[7], 71), 0)
    return {"right_side": right_side, "diagonal_inverse": diagonal_inverse, "lower_blocks": lower_blocks, "upper_blocks": upper_blocks, "row_level": row_level, "lower_links": lower_links, "upper_links": upper_links}


def reference(right_side, diagonal_inverse, lower_blocks, upper_blocks, row_level, lower_links, upper_links):
    ordering = jnp.argsort(row_level, stable=True).astype(jnp.int32)
    start = jnp.zeros(right_side.shape, right_side.dtype)

    def forward_row(carry, row_id):
        links = lower_links[row_id]
        present = links >= 0
        clamped = jnp.where(present, links, 0).astype(jnp.int32)
        pulled = jnp.zeros(right_side.shape[1:], jnp.float32)
        for slot_k in range(LINKS):
            product = jnp.dot(carry[clamped[slot_k]], lower_blocks[row_id, slot_k].T, preferred_element_type=jnp.float32)
            pulled = pulled + jnp.where(present[slot_k], product, jnp.zeros_like(product))
        reduced = (right_side[row_id].astype(jnp.float32) - pulled).astype(right_side.dtype)
        solved = jnp.dot(reduced, diagonal_inverse[row_id].T, preferred_element_type=jnp.float32).astype(right_side.dtype)
        return carry.at[row_id].set(solved), None

    forward, _ = lax.scan(forward_row, start, ordering)

    def backward_row(carry, row_id):
        links = upper_links[row_id]
        present = links >= 0
        clamped = jnp.where(present, links, 0).astype(jnp.int32)
        pulled = jnp.zeros(right_side.shape[1:], jnp.float32)
        for slot_k in range(LINKS):
            product = jnp.dot(carry[clamped[slot_k]], upper_blocks[row_id, slot_k].T, preferred_element_type=jnp.float32)
            pulled = pulled + jnp.where(present[slot_k], product, jnp.zeros_like(product))
        pushed = pulled.astype(right_side.dtype)
        solved = (forward[row_id].astype(jnp.float32) - jnp.dot(pushed, diagonal_inverse[row_id].T, preferred_element_type=jnp.float32)).astype(right_side.dtype)
        return carry.at[row_id].set(solved), None

    smoothed, _ = lax.scan(backward_row, start, ordering[::-1])
    return smoothed
```

```python
import functools

import jax
import jax.numpy as jnp
from jax import lax
from jax.experimental import pallas as pl
from jax.experimental.pallas import tpu as pltpu
from jax.sharding import PartitionSpec as P

LEVELS = 6
MOST_LEVEL = 3
LINKS = 3
FIELDS = 8

VMEM = pl.BlockSpec(memory_space=pltpu.VMEM)
SMEM = pl.BlockSpec(memory_space=pltpu.SMEM)


def swap_pairs(count):
    paired = [(i, i ^ 1) for i in range(count)]
    across = [(i, ((i + 1) ^ 1) - 1) for i in range(1, count - 1)]
    return paired, across


def exchange(value, count):
    paired, across = swap_pairs(count)
    return lax.ppermute(value, "blk", paired), lax.ppermute(value, "blk", across)


def gather_rows(shards, count):
    spread = jnp.broadcast_to(shards[None], (count,) + shards.shape)
    found = lax.all_to_all(spread, "line", 0, 0)
    found = jnp.transpose(found, (1, 2, 0, 3, 4))
    return found.reshape(shards.shape[:2] + (count * shards.shape[2], shards.shape[3]))


def table_kernel(level_ref, lower_ref, upper_ref, paired_ref, across_ref, table_ref):
    rows = level_ref.shape[0]
    me = lax.axis_index("blk")
    odd = lax.rem(me, 2)

    def source(target, first_level):
        rel = target - me * rows
        is_before, is_after = rel < 0, rel >= rows
        there = jnp.clip(jnp.where(is_before, rel + rows, rel - rows), 0, rows - 1)
        is_paired = jnp.where(odd == 1, is_before, is_after)
        paired_at = rows + paired_ref[there] - first_level
        across_at = rows + LEVELS - 1 + across_ref[there] - first_level
        beside = jnp.where(is_paired, paired_at, across_at)
        spot = jnp.where(is_before | is_after, beside, rel)
        return jnp.clip(spot, 0, rows + 2 * (LEVELS - 1) - 1)

    def one_level(level, _):
        first, second, third = jnp.int32(-1), jnp.int32(-1), jnp.int32(-1)
        for row in range(rows):
            hit = level_ref[row] == level
            third = jnp.where(hit & (second >= 0) & (third < 0), row, third)
            second = jnp.where(hit & (first >= 0) & (second < 0), row, second)
            first = jnp.where(hit & (first < 0), row, first)
        first = jnp.maximum(first, 0)
        second = jnp.where(second < 0, first, second)
        third = jnp.where(third < 0, first, third)
        for slot, row in enumerate((first, second, third)):
            base = (level * MOST_LEVEL + slot) * FIELDS
            table_ref[base] = row
            for k in range(LINKS):
                table_ref[base + 1 + k] = source(lower_ref[row * LINKS + k], 0)
                table_ref[base + 1 + LINKS + k] = source(upper_ref[row * LINKS + k], 1)
            table_ref[base + 1 + 2 * LINKS] = 0
        return 0

    lax.fori_loop(0, LEVELS, one_level, 0)


def times(x, block):
    return lax.dot_general(x, block, (((1,), (1,)), ((), ())), preferred_element_type=jnp.float32)


def pulled_of(pool_ref, blocks_ref, table_ref, base, row, field, first_block):
    spots = [table_ref[base + field + k] for k in range(LINKS)]
    x = jnp.concatenate([pool_ref[spot] for spot in spots], axis=1)
    blocks = jnp.concatenate([blocks_ref[row, first_block + k] for k in range(LINKS)], axis=1)
    return times(x, blocks)


def slots_of(table_ref, level):
    for slot in range(MOST_LEVEL):
        base = (level * MOST_LEVEL + slot) * FIELDS
        yield slot, base, table_ref[base]


def first_kernel(table_ref, side_ref, factors_ref, pool_ref, sent_ref):
    for slot, _, row in slots_of(table_ref, 0):
        solved = times(side_ref[row], factors_ref[row, 0]).astype(jnp.bfloat16)
        pool_ref[row] = solved
        if slot == 0:
            sent_ref[...] = solved


def forward_kernel(
    level, table_ref, side_ref, factors_ref, paired_ref, across_ref, old_ref, pool_ref, sent_ref
):
    rows = side_ref.shape[0]
    pool_ref[...] = old_ref[...]
    pool_ref[rows + level - 1] = paired_ref[...]
    pool_ref[rows + LEVELS - 1 + level - 1] = across_ref[...]
    solved_all = []
    for slot, base, row in slots_of(table_ref, level):
        pulled = pulled_of(pool_ref, factors_ref, table_ref, base, row, 1, 1)
        reduced = (side_ref[row].astype(jnp.float32) - pulled).astype(jnp.bfloat16)
        solved = times(reduced, factors_ref[row, 0]).astype(jnp.bfloat16)
        solved_all.append((row, solved))
    sent_ref[...] = solved_all[0][1]
    for row, solved in solved_all:
        pool_ref[row] = solved


def backward_kernel(
    level,
    table_ref,
    factors_ref,
    upper_ref,
    forward_ref,
    paired_ref,
    across_ref,
    old_ref,
    pool_ref,
    sent_ref,
):
    rows = factors_ref.shape[0]
    pool_ref[...] = old_ref[...]
    pool_ref[rows + level] = paired_ref[...]
    pool_ref[rows + LEVELS - 1 + level] = across_ref[...]
    if level == LEVELS - 2:
        for _, _, row in slots_of(table_ref, LEVELS - 1):
            pool_ref[row] = forward_ref[row]
    solved_all = []
    for slot, base, row in slots_of(table_ref, level):
        pulled = pulled_of(pool_ref, upper_ref, table_ref, base, row, 1 + LINKS, 0)
        pushed = pulled.astype(jnp.bfloat16)
        taken = times(pushed, factors_ref[row, 0])
        solved_all.append((row, (forward_ref[row].astype(jnp.float32) - taken).astype(jnp.bfloat16)))
    if level > 0:
        sent_ref[...] = solved_all[0][1]
    for row, solved in solved_all:
        pool_ref[row] = solved
    if level == 0:
        sent_ref[...] = pool_ref[pl.ds(0, rows)]


def local(
    right_side, diagonal_inverse, lower_blocks, upper_blocks, row_level, lower_links, upper_links
):
    rows, lines, variables = right_side.shape
    blk_count, line_count = lax.axis_size("blk"), lax.axis_size("line")
    pool_type = jax.ShapeDtypeStruct(
        (rows + 2 * (LEVELS - 1), lines, variables), jnp.bfloat16
    )
    row_type = jax.ShapeDtypeStruct((lines, variables), jnp.bfloat16)
    params = pltpu.CompilerParams(vmem_limit_bytes=32 * 1024 * 1024)

    near = jnp.concatenate([diagonal_inverse[:, None], lower_blocks], axis=1)
    factors = gather_rows(near, line_count)
    held_upper, factors = lax.optimization_barrier((upper_blocks, factors))
    upper = gather_rows(held_upper, line_count)

    paired_level, across_level = exchange(row_level, blk_count)
    table = pl.pallas_call(
        table_kernel,
        out_shape=jax.ShapeDtypeStruct((LEVELS * MOST_LEVEL * FIELDS,), jnp.int32),
        in_specs=[SMEM] * 5,
        out_specs=SMEM,
        name="table",
    )(row_level, lower_links.reshape(-1), upper_links.reshape(-1), paired_level, across_level)

    pool, sent = pl.pallas_call(
        first_kernel,
        out_shape=(pool_type, row_type),
        in_specs=[SMEM, VMEM, VMEM],
        out_specs=(VMEM, VMEM),
        compiler_params=params,
        name="forward0",
    )(table, right_side, factors)
    for level in range(1, LEVELS):
        paired, across = exchange(sent, blk_count)
        pool, sent = pl.pallas_call(
            functools.partial(forward_kernel, level),
            out_shape=(pool_type, row_type),
            in_specs=[SMEM] + [VMEM] * 5,
            out_specs=(VMEM, VMEM),
            compiler_params=params,
            name=f"forward{level}",
        )(table, right_side, factors, paired, across, pool)

    forward = pool
    pool = jnp.zeros(pool_type.shape, pool_type.dtype)
    for level in range(LEVELS - 2, -1, -1):
        paired, across = exchange(sent, blk_count)
        last = jax.ShapeDtypeStruct(right_side.shape, jnp.bfloat16)
        pool, sent = pl.pallas_call(
            functools.partial(backward_kernel, level),
            out_shape=(pool_type, row_type if level else last),
            in_specs=[SMEM] + [VMEM] * 6,
            out_specs=(VMEM, VMEM),
            compiler_params=params,
            name=f"backward{level}",
        )(table, factors, upper, forward, paired, across, pool)
    return sent


def solution(mesh):
    in_specs = (
        P("blk", "line", None),
        P("blk", "line", None),
        P("blk", None, "line", None),
        P("blk", None, "line", None),
        P("blk"),
        P("blk", None),
        P("blk", None),
    )
    out_specs = P("blk", "line", None)
    return jax.shard_map(local, mesh=mesh, in_specs=in_specs, out_specs=out_specs, check_vma=False)
```

```python
import functools

import jax
import jax.numpy as jnp
from jax import lax
from jax.experimental import pallas as pl
from jax.experimental.pallas import tpu as pltpu
from jax.sharding import PartitionSpec as P

LEVELS = 6
MOST_LEVEL = 3
LINKS = 3
TILE = 16
FIELDS = 8

VMEM = pl.BlockSpec(memory_space=pltpu.VMEM)
SMEM = pl.BlockSpec(memory_space=pltpu.SMEM)


def exchange(value, count):
    across = [(i, ((i + 1) ^ 1) - 1) for i in range(1, count - 1)]
    from_across = lax.ppermute(value, "blk", across)
    pairs = [[i, i + 1] for i in range(0, count, 2)]
    from_pair = lax.all_gather(value, "blk", axis=0, axis_index_groups=pairs)
    return from_pair, from_across


def gather_rows(shards, count):
    spread = jnp.broadcast_to(shards[None], (count,) + shards.shape)
    found = lax.all_to_all(spread, "line", 0, 0)
    found = jnp.transpose(found, (1, 2, 0, 3, 4))
    return found.reshape(shards.shape[:2] + (count * shards.shape[2], shards.shape[3]))


def rows_of_level(level_ref, level):
    first, second, third = jnp.int32(-1), jnp.int32(-1), jnp.int32(-1)
    for row in range(level_ref.shape[0]):
        hit = level_ref[row] == level
        third = jnp.where(hit & (second >= 0) & (third < 0), row, third)
        second = jnp.where(hit & (first >= 0) & (second < 0), row, second)
        first = jnp.where(hit & (first < 0), row, first)
    first = jnp.maximum(first, 0)
    second = jnp.where(second < 0, first, second)
    third = jnp.where(third < 0, first, third)
    return first, second, third


def table_kernel(level_ref, lower_ref, upper_ref, table_ref):
    rows = level_ref.shape[0]
    me = lax.axis_index("blk")
    odd = lax.rem(me, 2)

    def source(target):
        rel = target - me * rows
        is_before, is_after = rel < 0, rel >= rows
        there = jnp.where(is_before, rel + rows, rel - rows)
        is_paired = jnp.where(odd == 1, is_before, is_after)
        beside = there + jnp.where(is_paired, rows, 2 * rows)
        spot = jnp.where(is_before | is_after, beside, rel)
        return jnp.clip(spot, 0, 3 * rows - 1)

    def one_level(level, _):
        for slot, row in enumerate(rows_of_level(level_ref, level)):
            base = (level * MOST_LEVEL + slot) * FIELDS
            table_ref[base] = row
            for k in range(LINKS):
                table_ref[base + 1 + k] = source(lower_ref[row * LINKS + k])
                table_ref[base + 1 + LINKS + k] = source(upper_ref[row * LINKS + k])
            table_ref[base + 1 + 2 * LINKS] = 0
        return 0

    lax.fori_loop(0, LEVELS, one_level, 0)


def times(x, block):
    return lax.dot_general(x, block, (((1,), (1,)), ((), ())), preferred_element_type=jnp.float32)


def pulled_of(pool_ref, blocks_ref, table_ref, base, row, field, first_block):
    spots = [table_ref[base + field + k] for k in range(LINKS)]
    x = jnp.concatenate([pool_ref[spot] for spot in spots], axis=1)
    blocks = jnp.concatenate([blocks_ref[row, first_block + k] for k in range(LINKS)], axis=1)
    return times(x, blocks)


def slots_of(table_ref, level):
    for slot in range(MOST_LEVEL):
        base = (level * MOST_LEVEL + slot) * FIELDS
        yield slot, base, table_ref[base]


def send(sent_ref, row, solved):
    lines, variables = solved.shape
    sent_ref[pl.ds(0, lines)] = solved
    number = jnp.full((TILE, variables), row, jnp.int32).astype(jnp.float32)
    sent_ref[pl.ds(lines, TILE)] = number.astype(jnp.bfloat16)


def receive(pool_ref, old_ref, paired_ref, across_ref):
    lines, variables = pool_ref.shape[1:]
    rows = pool_ref.shape[0] // 3
    other = 1 - lax.rem(lax.axis_index("blk"), 2)
    for side, message in enumerate((paired_ref[other], across_ref[...])):
        value = message[:lines].reshape(lines // TILE, TILE, variables)
        number = message[lines:].astype(jnp.float32)
        for row in range(rows):
            spot = rows * (1 + side) + row
            if old_ref is None or old_ref.shape[0] == rows:
                pool_ref[spot] = message[:lines]
            else:
                hit = jnp.broadcast_to((number == row)[None], value.shape)
                old = old_ref[spot].reshape(value.shape)
                pool_ref[spot] = jnp.where(hit, value, old).reshape(lines, variables)
    if old_ref is not None:
        pool_ref[pl.ds(0, rows)] = old_ref[pl.ds(0, rows)]


def first_kernel(level_ref, side_ref, factors_ref, pool_ref, sent_ref):
    for slot, row in enumerate(rows_of_level(level_ref, 0)):
        solved = times(side_ref[row], factors_ref[row, 0]).astype(jnp.bfloat16)
        pool_ref[row] = solved
        if slot == 0:
            send(sent_ref, row, solved)


def forward_kernel(
    level, table_ref, side_ref, factors_ref, paired_ref, across_ref, old_ref, pool_ref, sent_ref
):
    receive(pool_ref, old_ref, paired_ref, across_ref)
    solved_all = []
    for slot, base, row in slots_of(table_ref, level):
        pulled = pulled_of(pool_ref, factors_ref, table_ref, base, row, 1, 1)
        reduced = (side_ref[row].astype(jnp.float32) - pulled).astype(jnp.bfloat16)
        solved = times(reduced, factors_ref[row, 0]).astype(jnp.bfloat16)
        solved_all.append((row, solved))
    send(sent_ref, *solved_all[0])
    for row, solved in solved_all:
        pool_ref[row] = solved


def backward_kernel(
    level, table_ref, factors_ref, upper_ref, forward_ref, paired_ref, across_ref, *rest
):
    pool_ref, sent_ref = rest[-2:]
    rows = factors_ref.shape[0]
    receive(pool_ref, rest[0] if len(rest) == 3 else None, paired_ref, across_ref)
    if level == LEVELS - 2:
        for _, _, row in slots_of(table_ref, LEVELS - 1):
            pool_ref[row] = forward_ref[row]
    solved_all = []
    for slot, base, row in slots_of(table_ref, level):
        pulled = pulled_of(pool_ref, upper_ref, table_ref, base, row, 1 + LINKS, 0)
        pushed = pulled.astype(jnp.bfloat16)
        taken = times(pushed, factors_ref[row, 0])
        solved_all.append((row, (forward_ref[row].astype(jnp.float32) - taken).astype(jnp.bfloat16)))
    if level > 0:
        send(sent_ref, *solved_all[0])
    for row, solved in solved_all:
        pool_ref[row] = solved
    if level == 0:
        sent_ref[...] = pool_ref[pl.ds(0, rows)]


def local(
    right_side, diagonal_inverse, lower_blocks, upper_blocks, row_level, lower_links, upper_links
):
    rows, lines, variables = right_side.shape
    blk_count, line_count = lax.axis_size("blk"), lax.axis_size("line")
    own_type = jax.ShapeDtypeStruct((rows, lines, variables), jnp.bfloat16)
    pool_type = jax.ShapeDtypeStruct((3 * rows, lines, variables), jnp.bfloat16)
    sent_type = jax.ShapeDtypeStruct((lines + TILE, variables), jnp.bfloat16)
    params = pltpu.CompilerParams(vmem_limit_bytes=32 * 1024 * 1024)

    near = jnp.concatenate([diagonal_inverse[:, None], lower_blocks], axis=1)
    factors = gather_rows(near, line_count)
    upper = gather_rows(upper_blocks, line_count)

    pool, sent = pl.pallas_call(
        first_kernel,
        out_shape=(own_type, sent_type),
        in_specs=[SMEM, VMEM, VMEM],
        out_specs=(VMEM, VMEM),
        compiler_params=params,
        name="forward0",
    )(row_level, right_side, factors)
    sent, lower_links, upper_links = lax.optimization_barrier((sent, lower_links, upper_links))
    table = pl.pallas_call(
        table_kernel,
        out_shape=jax.ShapeDtypeStruct((LEVELS * MOST_LEVEL * FIELDS,), jnp.int32),
        in_specs=[SMEM] * 3,
        out_specs=SMEM,
        name="table",
    )(row_level, lower_links.reshape(-1), upper_links.reshape(-1))
    for level in range(1, LEVELS):
        paired, across = exchange(sent, blk_count)
        pool, sent = pl.pallas_call(
            functools.partial(forward_kernel, level),
            out_shape=(pool_type, sent_type),
            in_specs=[SMEM] + [VMEM] * 5,
            out_specs=(VMEM, VMEM),
            compiler_params=params,
            name=f"forward{level}",
        )(table, right_side, factors, paired, across, pool)

    forward, held = pool, ()
    for level in range(LEVELS - 2, -1, -1):
        paired, across = exchange(sent, blk_count)
        pool, sent = pl.pallas_call(
            functools.partial(backward_kernel, level),
            out_shape=(pool_type, sent_type if level else own_type),
            in_specs=[SMEM] + [VMEM] * (5 + len(held)),
            out_specs=(VMEM, VMEM),
            compiler_params=params,
            name=f"backward{level}",
        )(table, factors, upper, forward, paired, across, *held)
        held = (pool,)
    return sent


def solution(mesh):
    in_specs = (
        P("blk", "line", None),
        P("blk", "line", None),
        P("blk", None, "line", None),
        P("blk", None, "line", None),
        P("blk"),
        P("blk", None),
        P("blk", None),
    )
    out_specs = P("blk", "line", None)
    return jax.shard_map(local, mesh=mesh, in_specs=in_specs, out_specs=out_specs, check_vma=False)
```

```python
import functools

import jax
import jax.numpy as jnp
from jax import lax
from jax.experimental import pallas as pl
from jax.experimental.pallas import tpu as pltpu
from jax.sharding import PartitionSpec as P

LEVELS = 6
MOST_LEVEL = 3
LINKS = 3
NEAR_ROWS = 9
TILE = 16
FIELDS = 8

VMEM = pl.BlockSpec(memory_space=pltpu.VMEM)
SMEM = pl.BlockSpec(memory_space=pltpu.SMEM)


def exchange(value, count):
    across = [(i, ((i + 1) ^ 1) - 1) for i in range(1, count - 1)]
    from_across = lax.ppermute(value, "blk", across)
    pairs = [[i, i + 1] for i in range(0, count, 2)]
    from_pair = lax.all_gather(value, "blk", axis=0, axis_index_groups=pairs)
    return from_pair, from_across


def gather_blocks(spread):
    found = lax.all_to_all(spread, "line", 0, 0)
    count, blocks, part, variables = found.shape
    return jnp.transpose(found, (1, 0, 2, 3)).reshape(blocks, count * part, variables)


def sort_rows(level_ref, order_ref):
    rows = level_ref.shape[0]
    keys = [level_ref[row] * rows + row for row in range(rows)]
    ranks = [jnp.int32(0)] * rows
    for row in range(rows):
        for other in range(row):
            is_less = (keys[other] < keys[row]).astype(jnp.int32)
            ranks[row] += is_less
            ranks[other] += 1 - is_less
    for row in range(rows):
        order_ref[ranks[row]] = row


def spread_near_kernel(level_ref, inverse_ref, lower_ref, out_ref, order_ref):
    sort_rows(level_ref, order_ref)
    for place in range(NEAR_ROWS):
        row = order_ref[place]
        parts = [inverse_ref[row]] + [lower_ref[row, k] for k in range(LINKS if place else 0)]
        for k, part in enumerate(parts):
            for device in range(out_ref.shape[0]):
                out_ref[device, first_block(place) + k] = part


def spread_far_kernel(level_ref, inverse_ref, lower_ref, upper_ref, out_ref, order_ref):
    sort_rows(level_ref, order_ref)
    rows = level_ref.shape[0]
    near, far = first_block(NEAR_ROWS), first_block(rows)
    for place in range(NEAR_ROWS, rows):
        row = order_ref[place]
        parts = [inverse_ref[row]] + [lower_ref[row, k] for k in range(LINKS)]
        for k, part in enumerate(parts):
            for device in range(out_ref.shape[0]):
                out_ref[device, first_block(place) - near + k] = part
    for place in range(rows - 1):
        row = order_ref[place]
        for k in range(LINKS):
            for device in range(out_ref.shape[0]):
                out_ref[device, far - near + LINKS * place + k] = upper_ref[row, k]


def rows_of_level(level_ref, level):
    first, second, third = jnp.int32(-1), jnp.int32(-1), jnp.int32(-1)
    for row in range(level_ref.shape[0]):
        hit = level_ref[row] == level
        third = jnp.where(hit & (second >= 0) & (third < 0), row, third)
        second = jnp.where(hit & (first >= 0) & (second < 0), row, second)
        first = jnp.where(hit & (first < 0), row, first)
    places = jnp.int32(0), (second >= 0).astype(jnp.int32), 2 * (third >= 0).astype(jnp.int32)
    first = jnp.maximum(first, 0)
    second = jnp.where(second < 0, first, second)
    third = jnp.where(third < 0, first, third)
    return tuple(zip((first, second, third), places))


def table_kernel(level_ref, lower_ref, upper_ref, table_ref):
    rows = level_ref.shape[0]
    me = lax.axis_index("blk")
    odd = lax.rem(me, 2)

    def source(target):
        rel = target - me * rows
        is_before, is_after = rel < 0, rel >= rows
        there = jnp.where(is_before, rel + rows, rel - rows)
        is_paired = jnp.where(odd == 1, is_before, is_after)
        beside = there + jnp.where(is_paired, rows, 2 * rows)
        spot = jnp.where(is_before | is_after, beside, rel)
        return jnp.clip(spot, 0, 3 * rows - 1)

    def one_level(level, start):
        found = rows_of_level(level_ref, level)
        for slot, (row, place) in enumerate(found):
            base = (level * MOST_LEVEL + slot) * FIELDS
            table_ref[base] = row
            for k in range(LINKS):
                table_ref[base + 1 + k] = source(lower_ref[row * LINKS + k])
                table_ref[base + 1 + LINKS + k] = source(upper_ref[row * LINKS + k])
            table_ref[base + 1 + 2 * LINKS] = jnp.minimum(start + place, rows - 1)
        return start + 1 + jnp.minimum(found[1][1], 1) + jnp.minimum(found[2][1], 1)

    lax.fori_loop(0, LEVELS, one_level, jnp.int32(0))


def times(x, block):
    return lax.dot_general(x, block, (((1,), (1,)), ((), ())), preferred_element_type=jnp.float32)


def first_block(place):
    return max(4 * place - 3, 0) if isinstance(place, int) else jnp.maximum(4 * place - 3, 0)


def block_of(near_ref, far_ref, index):
    near = near_ref.shape[0]
    if far_ref is None:
        return near_ref[index]
    far_block = far_ref[jnp.maximum(index - near, 0)]
    return jnp.where(index < near, near_ref[jnp.minimum(index, near - 1)], far_block)


def pulled_of(pool_ref, table_ref, base, field, blocks):
    spots = [table_ref[base + field + k] for k in range(LINKS)]
    x = jnp.concatenate([pool_ref[spot] for spot in spots], axis=1)
    return times(x, jnp.concatenate(blocks, axis=1))


def slots_of(table_ref, level):
    for slot in range(MOST_LEVEL):
        base = (level * MOST_LEVEL + slot) * FIELDS
        yield base, table_ref[base], table_ref[base + 1 + 2 * LINKS]


def send(sent_ref, row, solved):
    lines, variables = solved.shape
    sent_ref[pl.ds(0, lines)] = solved
    number = jnp.full((TILE, variables), row, jnp.int32).astype(jnp.float32)
    sent_ref[pl.ds(lines, TILE)] = number.astype(jnp.bfloat16)


def receive(pool_ref, old_ref, paired_ref, across_ref):
    lines, variables = pool_ref.shape[1:]
    rows = pool_ref.shape[0] // 3
    other = 1 - lax.rem(lax.axis_index("blk"), 2)
    for side, message in enumerate((paired_ref[other], across_ref[...])):
        value = message[:lines].reshape(lines // TILE, TILE, variables)
        number = message[lines:].astype(jnp.float32)
        for row in range(rows):
            spot = rows * (1 + side) + row
            if old_ref is None or old_ref.shape[0] == rows:
                pool_ref[spot] = message[:lines]
            else:
                hit = jnp.broadcast_to((number == row)[None], value.shape)
                old = old_ref[spot].reshape(value.shape)
                pool_ref[spot] = jnp.where(hit, value, old).reshape(lines, variables)
    if old_ref is not None:
        pool_ref[pl.ds(0, rows)] = old_ref[pl.ds(0, rows)]


def first_kernel(level_ref, side_ref, near_ref, pool_ref, sent_ref):
    for slot, (row, place) in enumerate(rows_of_level(level_ref, 0)):
        solved = times(side_ref[row], near_ref[first_block(place)]).astype(jnp.bfloat16)
        pool_ref[row] = solved
        if slot == 0:
            send(sent_ref, row, solved)


def forward_kernel(level, table_ref, side_ref, paired_ref, across_ref, old_ref, near_ref, *rest):
    pool_ref, sent_ref = rest[-2:]
    far_ref = rest[0] if len(rest) == 3 else None
    receive(pool_ref, old_ref, paired_ref, across_ref)
    solved_all = []
    for base, row, place in slots_of(table_ref, level):
        inverse_at = first_block(place)
        blocks = [block_of(near_ref, far_ref, inverse_at + 1 + k) for k in range(LINKS)]
        pulled = pulled_of(pool_ref, table_ref, base, 1, blocks)
        reduced = (side_ref[row].astype(jnp.float32) - pulled).astype(jnp.bfloat16)
        solved = times(reduced, block_of(near_ref, far_ref, inverse_at)).astype(jnp.bfloat16)
        solved_all.append((row, solved))
    send(sent_ref, *solved_all[0])
    for row, solved in solved_all:
        pool_ref[row] = solved


def backward_kernel(
    level, table_ref, near_ref, far_ref, forward_ref, paired_ref, across_ref, *rest
):
    pool_ref, sent_ref = rest[-2:]
    rows = pool_ref.shape[0] // 3
    receive(pool_ref, rest[0] if len(rest) == 3 else None, paired_ref, across_ref)
    if level == LEVELS - 2:
        for _, row, _ in slots_of(table_ref, LEVELS - 1):
            pool_ref[row] = forward_ref[row]
    solved_all = []
    for base, row, place in slots_of(table_ref, level):
        first_upper = first_block(rows) - near_ref.shape[0] + LINKS * place
        blocks = [far_ref[first_upper + k] for k in range(LINKS)]
        pulled = pulled_of(pool_ref, table_ref, base, 1 + LINKS, blocks)
        pushed = pulled.astype(jnp.bfloat16)
        taken = times(pushed, block_of(near_ref, far_ref, first_block(place)))
        solved_all.append((row, (forward_ref[row].astype(jnp.float32) - taken).astype(jnp.bfloat16)))
    if level > 0:
        send(sent_ref, *solved_all[0])
    for row, solved in solved_all:
        pool_ref[row] = solved
    if level == 0:
        sent_ref[...] = pool_ref[pl.ds(0, rows)]


def local(
    right_side, diagonal_inverse, lower_blocks, upper_blocks, row_level, lower_links, upper_links
):
    rows, lines, variables = right_side.shape
    blk_count, line_count = lax.axis_size("blk"), lax.axis_size("line")
    own_type = jax.ShapeDtypeStruct((rows, lines, variables), jnp.bfloat16)
    pool_type = jax.ShapeDtypeStruct((3 * rows, lines, variables), jnp.bfloat16)
    sent_type = jax.ShapeDtypeStruct((lines + TILE, variables), jnp.bfloat16)
    params = pltpu.CompilerParams(vmem_limit_bytes=32 * 1024 * 1024)

    def spread(kernel, blocks, *shards):
        part = diagonal_inverse.shape[1]
        return pl.pallas_call(
            kernel,
            out_shape=jax.ShapeDtypeStruct((line_count, blocks, part, variables), jnp.bfloat16),
            in_specs=[SMEM] + [VMEM] * len(shards),
            out_specs=VMEM,
            scratch_shapes=[pltpu.SMEM((rows,), jnp.int32)],
            compiler_params=params,
            name=kernel.__name__,
        )(row_level, *shards)

    near_count = first_block(NEAR_ROWS)
    far_count = first_block(rows) - near_count + LINKS * (rows - 1)
    near = gather_blocks(spread(spread_near_kernel, near_count, diagonal_inverse, lower_blocks))

    pool, sent = pl.pallas_call(
        first_kernel,
        out_shape=(own_type, sent_type),
        in_specs=[SMEM, VMEM, VMEM],
        out_specs=(VMEM, VMEM),
        compiler_params=params,
        name="forward0",
    )(row_level, right_side, near)
    sent, lower_links, upper_links, upper_blocks = lax.optimization_barrier(
        (sent, lower_links, upper_links, upper_blocks)
    )
    far_shards = diagonal_inverse, lower_blocks, upper_blocks
    far = gather_blocks(spread(spread_far_kernel, far_count, *far_shards))
    table = pl.pallas_call(
        table_kernel,
        out_shape=jax.ShapeDtypeStruct((LEVELS * MOST_LEVEL * FIELDS,), jnp.int32),
        in_specs=[SMEM] * 3,
        out_specs=SMEM,
        name="table",
    )(row_level, lower_links.reshape(-1), upper_links.reshape(-1))
    for level in range(1, LEVELS):
        paired, across = exchange(sent, blk_count)
        blocks = (near,) if level * MOST_LEVEL < NEAR_ROWS else (near, far)
        pool, sent = pl.pallas_call(
            functools.partial(forward_kernel, level),
            out_shape=(pool_type, sent_type),
            in_specs=[SMEM] + [VMEM] * (4 + len(blocks)),
            out_specs=(VMEM, VMEM),
            compiler_params=params,
            name=f"forward{level}",
        )(table, right_side, paired, across, pool, *blocks)

    forward, held = pool, ()
    for level in range(LEVELS - 2, -1, -1):
        paired, across = exchange(sent, blk_count)
        pool, sent = pl.pallas_call(
            functools.partial(backward_kernel, level),
            out_shape=(pool_type, sent_type if level else own_type),
            in_specs=[SMEM] + [VMEM] * (5 + len(held)),
            out_specs=(VMEM, VMEM),
            compiler_params=params,
            name=f"backward{level}",
        )(table, near, far, forward, paired, across, *held)
        held = (pool,)
    return sent


def solution(mesh):
    in_specs = (
        P("blk", "line", None),
        P("blk", "line", None),
        P("blk", None, "line", None),
        P("blk", None, "line", None),
        P("blk"),
        P("blk", None),
        P("blk", None),
    )
    out_specs = P("blk", "line", None)
    return jax.shard_map(local, mesh=mesh, in_specs=in_specs, out_specs=out_specs, check_vma=False)
```

```python
import functools

import jax
import jax.numpy as jnp
from jax import lax
from jax.experimental import pallas as pl
from jax.experimental.pallas import tpu as pltpu
from jax.sharding import PartitionSpec as P

LEVELS = 6
MOST_LEVEL = 3
LINKS = 3
NEAR_ROWS = 9
TILE = 16
LANES = 128
SPOT, ROW = 6, 4
LOWER, UPPER, KEY = 0, 1, 2

VMEM = pl.BlockSpec(memory_space=pltpu.VMEM)


def exchange(value, count):
    across = [(i, ((i + 1) ^ 1) - 1) for i in range(1, count - 1)]
    from_across = lax.ppermute(value, "blk", across)
    pairs = [[i, i + 1] for i in range(0, count, 2)]
    from_pair = lax.all_gather(value, "blk", axis=0, axis_index_groups=pairs)
    return from_pair, from_across


def first_block(place):
    return max(4 * place - 3, 0) if isinstance(place, int) else jnp.maximum(4 * place - 3, 0)


def prepare_kernel(rows, index_ref, shards_ref, near_ref, far_ref, table_ref):
    me = lax.axis_index("blk")
    paired_side = 1 - 2 * lax.rem(me, 2)

    across_of = lax.broadcasted_iota(jnp.int32, (TILE, LANES), 1)
    down_of = lax.broadcasted_iota(jnp.int32, (TILE, LANES), 0)
    index = index_ref[...]
    level = jnp.broadcast_to(jnp.where(across_of[:1] < rows, index[:1], LEVELS), (TILE, LANES))
    level_down = jnp.sum(jnp.where(across_of == down_of, level, 0), axis=1, keepdims=True)
    is_row = down_of < rows
    is_less = (level_down < level) & is_row
    is_same = (level_down == level) & (down_of < across_of) & is_row
    in_level = jnp.sum(is_same.astype(jnp.int32), axis=0, keepdims=True)
    place_of = jnp.sum(is_less.astype(jnp.int32), axis=0, keepdims=True) + in_level
    number = across_of[:1]

    def code(links):
        rel = links - me * rows
        side = (rel >= rows).astype(jnp.int32) - (rel < 0).astype(jnp.int32)
        there = rel - side * rows + jnp.where(side == paired_side, rows, 2 * rows)
        spot = jnp.clip(jnp.where(side == 0, rel, there), 0, 3 * rows - 1)
        packed = (number << (LINKS * SPOT)) | (place_of << (LINKS * SPOT + ROW))
        packed = packed | (1 << (LINKS * SPOT + 2 * ROW))
        for k in range(LINKS):
            packed = packed | (spot[k : k + 1] << (k * SPOT))
        return packed

    key = level[:1] * (MOST_LEVEL + 1) + in_level
    codes = [code(index[1 : 1 + LINKS]), code(index[1 + LINKS : 1 + 2 * LINKS]), key]
    table_ref[...] = jnp.concatenate(codes + [jnp.zeros_like(key)] * 5, axis=0)

    is_number = number < rows
    near, far = first_block(NEAR_ROWS), first_block(rows) - first_block(NEAR_ROWS)
    for place in range(rows):
        row = jnp.sum(jnp.where((place_of == place) & is_number, number, 0))
        for k in range(1 + LINKS if place else 1):
            block = first_block(place) + k
            if block < near:
                for device in range(near_ref.shape[0]):
                    near_ref[device, block] = shards_ref[row, k]
            else:
                far_ref[block - near] = shards_ref[row, k]
        for k in range(LINKS if place < rows - 1 else 0):
            far_ref[far + LINKS * place + k] = shards_ref[row, 1 + LINKS + k]


def times(x, block):
    return lax.dot_general(x, block, (((1,), (1,)), ((), ())), preferred_element_type=jnp.float32)


def block_at(gathered_ref, index):
    count, _, part, variables = gathered_ref.shape
    return gathered_ref[:, index].reshape(count * part, variables)


def block_of(near_ref, far_ref, index):
    near = near_ref.shape[1]
    if far_ref is None:
        return block_at(near_ref, index)
    far_block = block_at(far_ref, jnp.maximum(index - near, 0))
    return jnp.where(index < near, block_at(near_ref, jnp.minimum(index, near - 1)), far_block)


def slots_of(table_ref, level, kind):
    table = table_ref[...]
    found = []
    for slot in range(MOST_LEVEL):
        is_it = table[KEY : KEY + 1] == level * (MOST_LEVEL + 1) + slot
        code = jnp.sum(jnp.where(is_it, table[kind : kind + 1], 0))
        code = code if slot == 0 else jnp.where(code == 0, found[0], code)
        found.append(code)
    spot_mask, row_mask = (1 << SPOT) - 1, (1 << ROW) - 1
    return [
        (
            (code >> (LINKS * SPOT)) & row_mask,
            (code >> (LINKS * SPOT + ROW)) & row_mask,
            [(code >> (k * SPOT)) & spot_mask for k in range(LINKS)],
        )
        for code in found
    ]


def pulled_of(pool_ref, spots, blocks):
    x = jnp.concatenate([pool_ref[spot] for spot in spots], axis=1)
    return times(x, jnp.concatenate(blocks, axis=1))


def send(sent_ref, row, solved):
    lines, variables = solved.shape
    sent_ref[pl.ds(0, lines)] = solved
    number = jnp.full((TILE, variables), row, jnp.int32).astype(jnp.float32)
    sent_ref[pl.ds(lines, TILE)] = number.astype(jnp.bfloat16)


def lay_out(pool_ref, own, messages):
    rows, lines = own.shape[0], own.shape[1]
    pool_ref[pl.ds(0, rows)] = own[...]
    other = 1 - lax.rem(lax.axis_index("blk"), 2)
    for paired_ref, across_ref in zip(messages[::2], messages[1::2]):
        for side, message in enumerate((paired_ref.at[other], across_ref)):
            number = jnp.max(message[pl.ds(lines, TILE)].astype(jnp.float32)).astype(jnp.int32)
            pool_ref[rows * (1 + side) + number] = message[pl.ds(0, lines)]


def first_kernel(table_ref, side_ref, near_ref, own_ref, sent_ref):
    own_ref[...] = side_ref[...]
    for slot, (row, place, _) in enumerate(slots_of(table_ref, 0, LOWER)):
        solved = times(side_ref[row], block_at(near_ref, first_block(place))).astype(jnp.bfloat16)
        own_ref[row] = solved
        if slot == 0:
            send(sent_ref, row, solved)


def forward_kernel(level, table_ref, old_ref, near_ref, *rest):
    own_ref, sent_ref, pool_ref = rest[-3:]
    messages = rest[: 2 * level]
    far_ref = rest[2 * level] if len(rest) > 2 * level + 3 else None
    slots = slots_of(table_ref, level, LOWER)
    lay_out(pool_ref, old_ref, messages)
    own_ref[...] = old_ref[...]
    solved_all = []
    for row, place, spots in slots:
        inverse_at = first_block(place)
        blocks = [block_of(near_ref, far_ref, inverse_at + 1 + k) for k in range(LINKS)]
        pulled = pulled_of(pool_ref, spots, blocks)
        reduced = (old_ref[row].astype(jnp.float32) - pulled).astype(jnp.bfloat16)
        solved = times(reduced, block_of(near_ref, far_ref, inverse_at)).astype(jnp.bfloat16)
        solved_all.append((row, solved))
    send(sent_ref, *solved_all[0])
    for row, solved in solved_all:
        own_ref[row] = solved


def backward_kernel(level, table_ref, old_ref, near_ref, far_ref, *rest):
    rows = old_ref.shape[0]
    outs = rest[2 * (LEVELS - 1 - level) :]
    own_ref, sent_ref, pool_ref = outs if level else (outs[0], None, outs[1])
    slots = slots_of(table_ref, level, UPPER)
    lay_out(pool_ref, old_ref, rest[: 2 * (LEVELS - 1 - level)])
    own_ref[...] = old_ref[...]
    solved_all = []
    for row, place, spots in slots:
        first_upper = first_block(rows) - near_ref.shape[1] + LINKS * place
        blocks = [block_at(far_ref, first_upper + k) for k in range(LINKS)]
        pushed = pulled_of(pool_ref, spots, blocks).astype(jnp.bfloat16)
        taken = times(pushed, block_of(near_ref, far_ref, first_block(place)))
        solved_all.append((row, (old_ref[row].astype(jnp.float32) - taken).astype(jnp.bfloat16)))
    if level > 0:
        send(sent_ref, *solved_all[0])
    for row, solved in solved_all:
        own_ref[row] = solved


def local(
    right_side, diagonal_inverse, lower_blocks, upper_blocks, row_level, lower_links, upper_links
):
    rows, lines, variables = right_side.shape
    part = diagonal_inverse.shape[1]
    blk_count, line_count = lax.axis_size("blk"), lax.axis_size("line")
    own_type = jax.ShapeDtypeStruct((rows, lines, variables), jnp.bfloat16)
    sent_type = jax.ShapeDtypeStruct((lines + TILE, variables), jnp.bfloat16)
    pool = pltpu.VMEM((3 * rows, lines, variables), jnp.bfloat16)

    def call(name, kernel, out_shape, *args, scratch=(pool,)):
        return pl.pallas_call(
            kernel,
            out_shape=out_shape,
            in_specs=[VMEM] * len(args),
            out_specs=jax.tree.map(lambda _: VMEM, out_shape),
            scratch_shapes=scratch,
            compiler_params=pltpu.CompilerParams(vmem_limit_bytes=32 * 1024 * 1024),
            name=name,
        )(*args)

    index = jnp.concatenate([row_level[None], lower_links.T, upper_links.T], axis=0)
    index = jnp.pad(index, ((0, 8 - index.shape[0]), (0, LANES - rows)))
    shards = jnp.concatenate([diagonal_inverse[:, None], lower_blocks, upper_blocks], axis=1)
    near_count = first_block(NEAR_ROWS)
    far_count = first_block(rows) - near_count + LINKS * (rows - 1)
    near, far, table = call(
        "prepare",
        functools.partial(prepare_kernel, rows),
        (
            jax.ShapeDtypeStruct((line_count, near_count, part, variables), jnp.bfloat16),
            jax.ShapeDtypeStruct((far_count, part, variables), jnp.bfloat16),
            jax.ShapeDtypeStruct((8, LANES), jnp.int32),
        ),
        index,
        shards,
        scratch=(),
    )
    near = lax.all_to_all(near, "line", 0, 0)
    types = (own_type, sent_type)
    own, sent = call("forward0", first_kernel, types, table, right_side, near, scratch=())
    sent, far = lax.optimization_barrier((sent, far))
    far = lax.all_to_all(jnp.broadcast_to(far[None], (line_count,) + far.shape), "line", 0, 0)
    messages = ()
    for level in range(1, LEVELS):
        messages += exchange(sent, blk_count)
        args = (table, own, near) + messages
        if level * MOST_LEVEL >= NEAR_ROWS:
            args += (far,)
        kernel = functools.partial(forward_kernel, level)
        own, sent = call(f"forward{level}", kernel, types, *args)

    messages = ()
    for level in range(LEVELS - 2, -1, -1):
        messages += exchange(sent, blk_count)
        kernel = functools.partial(backward_kernel, level)
        args = (table, own, near, far) + messages
        own, *sent = call(f"backward{level}", kernel, types if level else (own_type,), *args)
        sent = sent[0] if level else None
    return own


def solution(mesh):
    in_specs = (
        P("blk", "line", None),
        P("blk", "line", None),
        P("blk", None, "line", None),
        P("blk", None, "line", None),
        P("blk"),
        P("blk", None),
        P("blk", None),
    )
    out_specs = P("blk", "line", None)
    return jax.shard_map(local, mesh=mesh, in_specs=in_specs, out_specs=out_specs, check_vma=False)
```

```python
import functools

import jax
import jax.numpy as jnp
from jax import lax
from jax.experimental import pallas as pl
from jax.experimental.pallas import tpu as pltpu
from jax.sharding import PartitionSpec as P

LEVELS = 6
MOST_LEVEL = 3
LINKS = 3
NEAR_ROWS = 10
TILE = 16
LANES = 128
SPOT, ROW = 6, 4
LOWER, UPPER, KEY = 0, 1, 2

VMEM = pl.BlockSpec(memory_space=pltpu.VMEM)


def from_pair(value, count):
    pairs = [[i, i + 1] for i in range(0, count, 2)]
    return lax.all_gather(value, "blk", axis=0, axis_index_groups=pairs)


def from_across(value, blk_count, line_count):
    groups = []
    for line in range(line_count):
        for blk in range(1, blk_count - 1, 2):
            groups.append([blk * line_count + line, (blk + 1) * line_count + line])
    for blk in (0, blk_count - 1):
        for line in range(0, line_count, 2):
            groups.append([blk * line_count + line, blk * line_count + line + 1])
    return lax.all_gather(value, ("blk", "line"), axis=0, axis_index_groups=groups)


def first_block(place):
    return max(4 * place - 3, 0) if isinstance(place, int) else jnp.maximum(4 * place - 3, 0)


def prepare_kernel(rows, index_ref, shards_ref, near_ref, far_ref, table_ref):
    me = lax.axis_index("blk")
    paired_side = 1 - 2 * lax.rem(me, 2)

    across_of = lax.broadcasted_iota(jnp.int32, (TILE, LANES), 1)
    down_of = lax.broadcasted_iota(jnp.int32, (TILE, LANES), 0)
    index = index_ref[...]
    level = jnp.broadcast_to(jnp.where(across_of[:1] < rows, index[:1], LEVELS), (TILE, LANES))
    level_down = jnp.sum(jnp.where(across_of == down_of, level, 0), axis=1, keepdims=True)
    is_row = down_of < rows
    is_less = (level_down < level) & is_row
    is_same = (level_down == level) & (down_of < across_of) & is_row
    in_level = jnp.sum(is_same.astype(jnp.int32), axis=0, keepdims=True)
    place_of = jnp.sum(is_less.astype(jnp.int32), axis=0, keepdims=True) + in_level
    number = across_of[:1]

    def code(links):
        rel = links - me * rows
        side = (rel >= rows).astype(jnp.int32) - (rel < 0).astype(jnp.int32)
        there = rel - side * rows + jnp.where(side == paired_side, rows, 2 * rows)
        spot = jnp.clip(jnp.where(side == 0, rel, there), 0, 3 * rows - 1)
        packed = (number << (LINKS * SPOT)) | (place_of << (LINKS * SPOT + ROW))
        packed = packed | (1 << (LINKS * SPOT + 2 * ROW))
        for k in range(LINKS):
            packed = packed | (spot[k : k + 1] << (k * SPOT))
        return packed

    key = level[:1] * (MOST_LEVEL + 1) + in_level
    codes = [code(index[1 : 1 + LINKS]), code(index[1 + LINKS : 1 + 2 * LINKS]), key]
    table_ref[...] = jnp.concatenate(codes + [jnp.zeros_like(key)] * 5, axis=0)

    is_number = number < rows
    near, far = first_block(NEAR_ROWS), first_block(rows) - first_block(NEAR_ROWS)
    for place in range(rows):
        row = jnp.sum(jnp.where((place_of == place) & is_number, number, 0))
        for k in range(1 + LINKS if place else 1):
            block = first_block(place) + k
            if block < near:
                for device in range(near_ref.shape[0]):
                    near_ref[device, block] = shards_ref[row, k]
            else:
                far_ref[block - near] = shards_ref[row, k]
        for k in range(LINKS if place < rows - 1 else 0):
            far_ref[far + LINKS * place + k] = shards_ref[row, 1 + LINKS + k]


def times(x, block):
    return lax.dot_general(x, block, (((1,), (1,)), ((), ())), preferred_element_type=jnp.float32)


def block_at(gathered_ref, index):
    count, _, part, variables = gathered_ref.shape
    return gathered_ref[:, index].reshape(count * part, variables)


def block_of(near_ref, far_ref, index):
    near = near_ref.shape[1]
    if far_ref is None:
        return block_at(near_ref, index)
    far_block = block_at(far_ref, jnp.maximum(index - near, 0))
    return jnp.where(index < near, block_at(near_ref, jnp.minimum(index, near - 1)), far_block)


def slots_of(table_ref, level, kind, count=MOST_LEVEL):
    table = table_ref[...]
    found = []
    for slot in range(count):
        is_it = table[KEY : KEY + 1] == level * (MOST_LEVEL + 1) + slot
        code = jnp.sum(jnp.where(is_it, table[kind : kind + 1], 0))
        code = code if slot == 0 else jnp.where(code == 0, found[0], code)
        found.append(code)
    spot_mask, row_mask = (1 << SPOT) - 1, (1 << ROW) - 1
    return [
        (
            (code >> (LINKS * SPOT)) & row_mask,
            (code >> (LINKS * SPOT + ROW)) & row_mask,
            [(code >> (k * SPOT)) & spot_mask for k in range(LINKS)],
        )
        for code in found
    ]


def joined(parts):
    return jnp.concatenate(parts, axis=1)


def put_message(ref, value, number):
    lines, variables = value.shape
    ref[pl.ds(0, lines)] = value
    number = jnp.full((TILE, variables), number, jnp.int32).astype(jnp.float32)
    ref[pl.ds(lines, TILE)] = number.astype(jnp.bfloat16)


def number_in(ref, lines):
    return jnp.max(ref[pl.ds(lines, TILE)].astype(jnp.float32)).astype(jnp.int32)


def lay_out(pool_ref, own_ref, paired_refs, across_refs):
    rows, lines = own_ref.shape[0], own_ref.shape[1]
    pool_ref[pl.ds(0, rows)] = own_ref[...]
    other = 1 - lax.rem(lax.axis_index("blk"), 2)
    for ref in paired_refs:
        message = ref.at[other]
        pool_ref[rows + number_in(message, lines)] = message[pl.ds(0, lines)]
    numbers = []
    for ref in across_refs:
        numbers.append(number_in(ref, lines))
        pool_ref[2 * rows + numbers[-1]] = ref[pl.ds(0, lines)]
    return numbers


def blocks_for(kind, rows, near_ref, far_ref, place):
    if kind == LOWER:
        first = first_block(place) + 1
        return [block_of(near_ref, far_ref, first + k) for k in range(LINKS)]
    first = first_block(rows) - near_ref.shape[1] + LINKS * place
    return [block_at(far_ref, first + k) for k in range(LINKS)]


def solve(kind, start, pulled, inverse):
    if kind == LOWER:
        reduced = (start.astype(jnp.float32) - pulled).astype(jnp.bfloat16)
        return times(reduced, inverse).astype(jnp.bfloat16)
    taken = times(pulled.astype(jnp.bfloat16), inverse)
    return (start.astype(jnp.float32) - taken).astype(jnp.bfloat16)


def first_kernel(table_ref, side_ref, near_ref, own_ref, sent_ref):
    own_ref[...] = side_ref[...]
    for slot, (row, place, _) in enumerate(slots_of(table_ref, 0, LOWER)):
        solved = times(side_ref[row], block_at(near_ref, first_block(place))).astype(jnp.bfloat16)
        own_ref[row] = solved
        if slot == 0:
            put_message(sent_ref, solved, row)


def ahead_kernel(kind, level, count, *refs):
    count_paired, count_across, count_blocks = count
    table_ref, own_ref, sent_ref = refs[:3]
    refs = refs[3:]
    paired_refs, refs = refs[:count_paired], refs[count_paired:]
    across_refs, refs = refs[:count_across], refs[count_across:]
    near_ref, far_ref = refs[0], refs[1] if count_blocks == 2 else None
    out_ref, pool_ref = refs[-2:]
    rows, lines = own_ref.shape[0], own_ref.shape[1]
    row, place, spots = slots_of(table_ref, level, kind, 1)[0]
    numbers = lay_out(pool_ref, own_ref, paired_refs, across_refs)
    blocks = blocks_for(kind, rows, near_ref, far_ref, place)
    sources, lacking = [], jnp.zeros(blocks[0].shape, jnp.float32)
    for spot, block in zip(spots, blocks):
        is_lacking = spot >= 2 * rows
        for number in numbers:
            is_lacking &= spot != 2 * rows + number
        source = pool_ref[spot]
        sources.append(jnp.where(is_lacking, jnp.zeros_like(source), source))
        lacking += jnp.where(is_lacking, block, jnp.zeros_like(block)).astype(jnp.float32)
    known = times(joined(sources), joined(blocks))
    if kind == LOWER:
        known = own_ref[row].astype(jnp.float32) - known
    variables = known.shape[1]
    number = number_in(sent_ref, lines) + TILE * row
    out_ref[pl.ds(0, lines)] = sent_ref[pl.ds(0, lines)]
    tile = jnp.full((TILE, variables), number, jnp.int32).astype(jnp.float32)
    out_ref[pl.ds(lines, TILE)] = tile.astype(jnp.bfloat16)
    out_ref[pl.ds(lines + TILE, lines)] = known.astype(jnp.bfloat16)
    out_ref[pl.ds(2 * lines + TILE, variables)] = lacking.astype(jnp.bfloat16)
    inverse = block_of(near_ref, far_ref, first_block(place))
    out_ref[pl.ds(2 * lines + TILE + variables, variables)] = inverse


def level_kernel(kind, level, count, *refs):
    count_paired, count_across, count_blocks, has_message, has_start = count
    table_ref, old_ref = refs[:2]
    refs = refs[2:]
    paired_refs, refs = refs[:count_paired], refs[count_paired:]
    across_refs, refs = refs[:count_across], refs[count_across:]
    near_ref, far_ref = refs[0], refs[1] if count_blocks == 2 else None
    refs = refs[count_blocks:]
    pool_ref = refs[-1]
    rows, lines, variables = old_ref.shape
    slots = slots_of(table_ref, level, kind)
    lay_out(pool_ref, old_ref, paired_refs, across_refs)
    if has_message:
        message_ref, refs = refs[0], refs[1:]
        start_ref, refs = (refs[0], refs[1:]) if has_start else (None, refs)
        own_ref, sent_ref, now_ref, next_ref = refs[:-1]
        mine = 1 - lax.rem(lax.axis_index("blk"), 2)
        message = message_ref.at[1 - mine]
        numbers = number_in(message, lines)
        number_next = numbers // TILE
        number_now = numbers - TILE * number_next
        across_now = message[pl.ds(0, lines)]
        pool_ref[2 * rows + number_now] = across_now
        put_message(now_ref, across_now, number_now)
        known = message[pl.ds(lines + TILE, lines)]
        lacking = message[pl.ds(2 * lines + TILE, variables)]
        inverse = message[pl.ds(2 * lines + TILE + variables, variables)]
        added = times(message_ref[mine, pl.ds(0, lines)], lacking)
        if kind == LOWER:
            across_next = solve(kind, known, added, inverse)
        else:
            start = start_ref[pl.ds(0, lines)]
            across_next = solve(kind, start, known.astype(jnp.float32) + added, inverse)
        put_message(next_ref, across_next, number_next)
    else:
        own_ref, sent_ref = refs[:-1] if len(refs) == 3 else (refs[0], None)
    own_ref[...] = old_ref[...]
    solved_all = []
    for row, place, spots in slots:
        blocks = blocks_for(kind, rows, near_ref, far_ref, place)
        pulled = times(joined([pool_ref[spot] for spot in spots]), joined(blocks))
        inverse = block_of(near_ref, far_ref, first_block(place))
        solved_all.append((row, solve(kind, old_ref[row], pulled, inverse)))
    if sent_ref is not None:
        put_message(sent_ref, solved_all[0][1], solved_all[0][0])
    for row, solved in solved_all:
        own_ref[row] = solved


def local(
    right_side, diagonal_inverse, lower_blocks, upper_blocks, row_level, lower_links, upper_links
):
    rows, lines, variables = right_side.shape
    part = diagonal_inverse.shape[1]
    blk_count, line_count = lax.axis_size("blk"), lax.axis_size("line")
    own_type = jax.ShapeDtypeStruct((rows, lines, variables), jnp.bfloat16)
    sent_type = jax.ShapeDtypeStruct((lines + TILE, variables), jnp.bfloat16)
    pool = pltpu.VMEM((3 * rows, lines, variables), jnp.bfloat16)

    def call(name, kernel, out_shape, *args, scratch=(pool,)):
        return pl.pallas_call(
            kernel,
            out_shape=out_shape,
            in_specs=[VMEM] * len(args),
            out_specs=jax.tree.map(lambda _: VMEM, out_shape),
            scratch_shapes=scratch,
            compiler_params=pltpu.CompilerParams(vmem_limit_bytes=32 * 1024 * 1024),
            name=name,
        )(*args)

    side = right_side
    index = jnp.concatenate([row_level[None], lower_links.T, upper_links.T], axis=0)
    index = jnp.pad(index, ((0, 8 - index.shape[0]), (0, LANES - rows)))
    shards = jnp.concatenate([diagonal_inverse[:, None], lower_blocks, upper_blocks], axis=1)
    near_count = first_block(NEAR_ROWS)
    far_count = first_block(rows) - near_count + LINKS * (rows - 1)
    near, far, table = call(
        "prepare",
        functools.partial(prepare_kernel, rows),
        (
            jax.ShapeDtypeStruct((line_count, near_count, part, variables), jnp.bfloat16),
            jax.ShapeDtypeStruct((far_count, part, variables), jnp.bfloat16),
            jax.ShapeDtypeStruct((8, LANES), jnp.int32),
        ),
        index,
        shards,
        scratch=(),
    )
    near = lax.all_to_all(near, "line", 0, 0)
    types = (own_type, sent_type)
    own, sent = call("forward0", first_kernel, types, table, side, near, scratch=())
    sent, far = lax.optimization_barrier((sent, far))
    far = lax.all_to_all(jnp.broadcast_to(far[None], (line_count,) + far.shape), "line", 0, 0)
    message_type = jax.ShapeDtypeStruct((2 * lines + TILE + 2 * variables, variables), jnp.bfloat16)

    def ahead(name, kind, level, own, sent, paired, across, blocks):
        count = len(paired), len(across), len(blocks)
        kernel = functools.partial(ahead_kernel, kind, level, count)
        args = (table, own, sent, *paired, *across, *blocks)
        return from_across(call(name, kernel, message_type, *args), blk_count, line_count)

    def step(name, kind, level, own, paired, across, blocks, message=None, start=None):
        extra = tuple(x for x in (message, start) if x is not None)
        count = len(paired), len(across), len(blocks), message is not None, start is not None
        kernel = functools.partial(level_kernel, kind, level, count)
        outs = (own_type,)
        if kind == LOWER or level > 0:
            outs += (sent_type,)
        if message is not None:
            outs += (sent_type, sent_type)
        return call(name, kernel, outs, table, own, *paired, *across, *blocks, *extra)

    paired, across, ahead_of = (from_pair(sent, blk_count),), (), {}
    for level in range(1, LEVELS, 2):
        blocks = (near,) if level + 1 < LEVELS // 2 else (near, far)
        held = (near,) if level <= 3 else blocks
        message = ahead(f"ahead{level}", LOWER, level, own, sent, paired, across, held)
        args = own, paired, across, blocks, message
        own, sent, now, ahead_of[level] = step(f"forward{level}", LOWER, level, *args)
        across += (now, ahead_of[level])
        paired += (from_pair(sent, blk_count),)
        if level + 1 < LEVELS:
            args = own, paired, across, blocks
            own, sent = step(f"forward{level + 1}", LOWER, level + 1, *args)
            paired += (from_pair(sent, blk_count),)

    paired, across, blocks = paired[-1:], across[-1:], (near, far)
    for level in range(LEVELS - 2, -1, -2):
        own, *sent = step(f"backward{level}", UPPER, level, own, paired, across, blocks)
        if level == 0:
            break
        paired += (from_pair(sent[0], blk_count),)
        ahead_args = own, sent[0], paired, across, blocks
        message = ahead(f"behind{level - 1}", UPPER, level - 1, *ahead_args)
        args = own, paired, across, blocks, message, ahead_of[level - 1]
        own, sent, now, following = step(f"backward{level - 1}", UPPER, level - 1, *args)
        across += (now, following)
        paired += (from_pair(sent, blk_count),)
    return own


def solution(mesh):
    in_specs = (
        P("blk", "line", None),
        P("blk", "line", None),
        P("blk", None, "line", None),
        P("blk", None, "line", None),
        P("blk"),
        P("blk", None),
        P("blk", None),
    )
    out_specs = P("blk", "line", None)
    return jax.shard_map(local, mesh=mesh, in_specs=in_specs, out_specs=out_specs, check_vma=False)
```

```python
import functools

import jax
import jax.numpy as jnp
from jax import lax
from jax.experimental import pallas as pl
from jax.experimental.pallas import tpu as pltpu
from jax.sharding import PartitionSpec as P

LEVELS = 6
MOST_LEVEL = 3
LINKS = 3
NEAR_ROWS = 10
TILE = 16
LANES = 128
SPOT, ROW = 6, 4
LOWER, UPPER, KEY = 0, 1, 2

VMEM = pl.BlockSpec(memory_space=pltpu.VMEM)


def from_pair(value, count):
    pairs = [[i, i + 1] for i in range(0, count, 2)]
    return lax.all_gather(value, "blk", axis=0, axis_index_groups=pairs)


def from_across(value, blk_count, line_count):
    groups = []
    for line in range(line_count):
        for blk in range(1, blk_count - 1, 2):
            groups.append([blk * line_count + line, (blk + 1) * line_count + line])
    for blk in (0, blk_count - 1):
        for line in range(0, line_count, 2):
            groups.append([blk * line_count + line, blk * line_count + line + 1])
    return lax.all_gather(value, ("blk", "line"), axis=0, axis_index_groups=groups)


def first_block(place):
    return max(4 * place - 3, 0) if isinstance(place, int) else jnp.maximum(4 * place - 3, 0)


def prepare_kernel(rows, index_ref, shards_ref, near_ref, far_ref, table_ref):
    me = lax.axis_index("blk")
    paired_side = 1 - 2 * lax.rem(me, 2)

    across_of = lax.broadcasted_iota(jnp.int32, (TILE, LANES), 1)
    down_of = lax.broadcasted_iota(jnp.int32, (TILE, LANES), 0)
    index = index_ref[...]
    level = jnp.broadcast_to(jnp.where(across_of[:1] < rows, index[:1], LEVELS), (TILE, LANES))
    level_down = jnp.sum(jnp.where(across_of == down_of, level, 0), axis=1, keepdims=True)
    is_row = down_of < rows
    is_less = (level_down < level) & is_row
    is_same = (level_down == level) & (down_of < across_of) & is_row
    in_level = jnp.sum(is_same.astype(jnp.int32), axis=0, keepdims=True)
    place_of = jnp.sum(is_less.astype(jnp.int32), axis=0, keepdims=True) + in_level
    number = across_of[:1]

    def code(links):
        rel = links - me * rows
        side = (rel >= rows).astype(jnp.int32) - (rel < 0).astype(jnp.int32)
        there = rel - side * rows + jnp.where(side == paired_side, rows, 2 * rows)
        spot = jnp.clip(jnp.where(side == 0, rel, there), 0, 3 * rows - 1)
        packed = (number << (LINKS * SPOT)) | (place_of << (LINKS * SPOT + ROW))
        packed = packed | (1 << (LINKS * SPOT + 2 * ROW))
        for k in range(LINKS):
            packed = packed | (spot[k : k + 1] << (k * SPOT))
        return packed

    key = level[:1] * (MOST_LEVEL + 1) + in_level
    codes = [code(index[1 : 1 + LINKS]), code(index[1 + LINKS : 1 + 2 * LINKS]), key]
    table_ref[...] = jnp.concatenate(codes + [jnp.zeros_like(key)] * 5, axis=0)

    is_number = number < rows
    near, far = first_block(NEAR_ROWS), first_block(rows) - first_block(NEAR_ROWS)
    for place in range(rows):
        row = jnp.sum(jnp.where((place_of == place) & is_number, number, 0))
        for k in range(1 + LINKS if place else 1):
            block = first_block(place) + k
            if block < near:
                for device in range(near_ref.shape[0]):
                    near_ref[device, block] = shards_ref[row, k]
            else:
                far_ref[block - near] = shards_ref[row, k]
        for k in range(LINKS if place < rows - 1 else 0):
            far_ref[far + LINKS * place + k] = shards_ref[row, 1 + LINKS + k]


def times(x, block):
    return lax.dot_general(x, block, (((1,), (1,)), ((), ())), preferred_element_type=jnp.float32)


def block_at(gathered_ref, index):
    count, _, part, variables = gathered_ref.shape
    return gathered_ref[:, index].reshape(count * part, variables)


def block_of(near_ref, far_ref, index):
    near = near_ref.shape[1]
    if far_ref is None:
        return block_at(near_ref, index)
    far_block = block_at(far_ref, jnp.maximum(index - near, 0))
    return jnp.where(index < near, block_at(near_ref, jnp.minimum(index, near - 1)), far_block)


def slots_of(table_ref, level, kind, count=MOST_LEVEL):
    table = table_ref[...]
    found = []
    for slot in range(count):
        is_it = table[KEY : KEY + 1] == level * (MOST_LEVEL + 1) + slot
        code = jnp.sum(jnp.where(is_it, table[kind : kind + 1], 0))
        code = code if slot == 0 else jnp.where(code == 0, found[0], code)
        found.append(code)
    spot_mask, row_mask = (1 << SPOT) - 1, (1 << ROW) - 1
    return [
        (
            (code >> (LINKS * SPOT)) & row_mask,
            (code >> (LINKS * SPOT + ROW)) & row_mask,
            [(code >> (k * SPOT)) & spot_mask for k in range(LINKS)],
        )
        for code in found
    ]


def joined(parts):
    return jnp.concatenate(parts, axis=1)


def put_message(ref, value, number):
    lines, variables = value.shape
    ref[pl.ds(0, lines)] = value
    number = jnp.full((TILE, variables), number, jnp.int32).astype(jnp.float32)
    ref[pl.ds(lines, TILE)] = number.astype(jnp.bfloat16)


def number_in(ref, lines):
    return jnp.max(ref[pl.ds(lines, TILE)].astype(jnp.float32)).astype(jnp.int32)


def lay_out(pool_ref, own_ref, paired_refs, across_refs):
    rows, lines = own_ref.shape[0], own_ref.shape[1]
    pool_ref[pl.ds(0, rows)] = own_ref[...]
    other = 1 - lax.rem(lax.axis_index("blk"), 2)
    for ref in paired_refs:
        message = ref.at[other]
        pool_ref[rows + number_in(message, lines)] = message[pl.ds(0, lines)]
    numbers = []
    for ref in across_refs:
        numbers.append(number_in(ref, lines))
        pool_ref[2 * rows + numbers[-1]] = ref[pl.ds(0, lines)]
    return numbers


def blocks_for(kind, rows, near_ref, far_ref, place):
    if kind == LOWER:
        first = first_block(place) + 1
        return [block_of(near_ref, far_ref, first + k) for k in range(LINKS)]
    first = first_block(rows) - near_ref.shape[1] + LINKS * place
    return [block_at(far_ref, first + k) for k in range(LINKS)]


def solve(kind, start, pulled, inverse):
    if kind == LOWER:
        reduced = (start.astype(jnp.float32) - pulled).astype(jnp.bfloat16)
        return times(reduced, inverse).astype(jnp.bfloat16)
    taken = times(pulled.astype(jnp.bfloat16), inverse)
    return (start.astype(jnp.float32) - taken).astype(jnp.bfloat16)


def first_kernel(table_ref, side_ref, near_ref, own_ref, sent_ref):
    own_ref[...] = side_ref[...]
    for slot, (row, place, _) in enumerate(slots_of(table_ref, 0, LOWER)):
        solved = times(side_ref[row], block_at(near_ref, first_block(place))).astype(jnp.bfloat16)
        own_ref[row] = solved
        if slot == 0:
            put_message(sent_ref, solved, row)


def ahead_kernel(kind, level, count, *refs):
    count_paired, count_across, count_blocks = count
    table_ref, own_ref, sent_ref = refs[:3]
    refs = refs[3:]
    paired_refs, refs = refs[:count_paired], refs[count_paired:]
    across_refs, refs = refs[:count_across], refs[count_across:]
    near_ref, far_ref = refs[0], refs[1] if count_blocks == 2 else None
    out_ref, pool_ref = refs[-2:]
    rows, lines = own_ref.shape[0], own_ref.shape[1]
    row, place, spots = slots_of(table_ref, level, kind, 1)[0]
    numbers = lay_out(pool_ref, own_ref, paired_refs, across_refs)
    blocks = blocks_for(kind, rows, near_ref, far_ref, place)
    sources, lacking = [], jnp.zeros(blocks[0].shape, jnp.float32)
    for spot, block in zip(spots, blocks):
        is_lacking = spot >= 2 * rows
        for number in numbers:
            is_lacking &= spot != 2 * rows + number
        source = pool_ref[spot]
        sources.append(jnp.where(is_lacking, jnp.zeros_like(source), source))
        lacking += jnp.where(is_lacking, block, jnp.zeros_like(block)).astype(jnp.float32)
    known = times(joined(sources), joined(blocks))
    if kind == LOWER:
        known = own_ref[row].astype(jnp.float32) - known
    variables = known.shape[1]
    number = number_in(sent_ref, lines) + TILE * row
    out_ref[pl.ds(0, lines)] = sent_ref[pl.ds(0, lines)]
    tile = jnp.full((TILE, variables), number, jnp.int32).astype(jnp.float32)
    out_ref[pl.ds(lines, TILE)] = tile.astype(jnp.bfloat16)
    out_ref[pl.ds(lines + TILE, lines)] = known.astype(jnp.bfloat16)
    out_ref[pl.ds(2 * lines + TILE, variables)] = lacking.astype(jnp.bfloat16)
    inverse = block_of(near_ref, far_ref, first_block(place))
    out_ref[pl.ds(2 * lines + TILE + variables, variables)] = inverse


def level_kernel(kind, level, count, *refs):
    count_paired, count_across, count_blocks, has_message, has_start, gives_now = count
    table_ref, old_ref = refs[:2]
    refs = refs[2:]
    paired_refs, refs = refs[:count_paired], refs[count_paired:]
    across_refs, refs = refs[:count_across], refs[count_across:]
    near_ref, far_ref = refs[0], refs[1] if count_blocks == 2 else None
    refs = refs[count_blocks:]
    pool_ref = refs[-1]
    rows, lines, variables = old_ref.shape
    slots = slots_of(table_ref, level, kind)
    lay_out(pool_ref, old_ref, paired_refs, across_refs)
    if has_message:
        message, mine_ref, refs = refs[0], refs[1], refs[2:]
        start_ref, refs = (refs[0], refs[1:]) if has_start else (None, refs)
        own_ref, sent_ref, next_ref = refs[:3]
        if len(message.shape) == 3:
            message = message.at[lax.rem(lax.axis_index("blk"), 2)]
        numbers = number_in(message, lines)
        number_next = numbers // TILE
        number_now = numbers - TILE * number_next
        across_now = message[pl.ds(0, lines)]
        pool_ref[2 * rows + number_now] = across_now
        if gives_now:
            put_message(refs[3], across_now, number_now)
        known = message[pl.ds(lines + TILE, lines)]
        lacking = message[pl.ds(2 * lines + TILE, variables)]
        inverse = message[pl.ds(2 * lines + TILE + variables, variables)]
        added = times(mine_ref[pl.ds(0, lines)], lacking)
        if kind == LOWER:
            across_next = solve(kind, known, added, inverse)
        else:
            start = start_ref[pl.ds(0, lines)]
            across_next = solve(kind, start, known.astype(jnp.float32) + added, inverse)
        put_message(next_ref, across_next, number_next)
    else:
        own_ref, sent_ref = refs[:-1] if len(refs) == 3 else (refs[0], None)
    own_ref[...] = old_ref[...]
    solved_all = []
    for row, place, spots in slots:
        blocks = blocks_for(kind, rows, near_ref, far_ref, place)
        pulled = times(joined([pool_ref[spot] for spot in spots]), joined(blocks))
        inverse = block_of(near_ref, far_ref, first_block(place))
        solved_all.append((row, solve(kind, old_ref[row], pulled, inverse)))
    if sent_ref is not None:
        put_message(sent_ref, solved_all[0][1], solved_all[0][0])
    for row, solved in solved_all:
        own_ref[row] = solved


def local(
    right_side, diagonal_inverse, lower_blocks, upper_blocks, row_level, lower_links, upper_links
):
    rows, lines, variables = right_side.shape
    part = diagonal_inverse.shape[1]
    blk_count, line_count = lax.axis_size("blk"), lax.axis_size("line")
    own_type = jax.ShapeDtypeStruct((rows, lines, variables), jnp.bfloat16)
    sent_type = jax.ShapeDtypeStruct((lines + TILE, variables), jnp.bfloat16)
    pool = pltpu.VMEM((3 * rows, lines, variables), jnp.bfloat16)

    def call(name, kernel, out_shape, *args, scratch=(pool,)):
        return pl.pallas_call(
            kernel,
            out_shape=out_shape,
            in_specs=[VMEM] * len(args),
            out_specs=jax.tree.map(lambda _: VMEM, out_shape),
            scratch_shapes=scratch,
            compiler_params=pltpu.CompilerParams(vmem_limit_bytes=32 * 1024 * 1024),
            name=name,
        )(*args)

    side = right_side
    index = jnp.concatenate([row_level[None], lower_links.T, upper_links.T], axis=0)
    index = jnp.pad(index, ((0, 8 - index.shape[0]), (0, LANES - rows)))
    shards = jnp.concatenate([diagonal_inverse[:, None], lower_blocks, upper_blocks], axis=1)
    near_count = first_block(NEAR_ROWS)
    far_count = first_block(rows) - near_count + LINKS * (rows - 1)
    near, far, table = call(
        "prepare",
        functools.partial(prepare_kernel, rows),
        (
            jax.ShapeDtypeStruct((line_count, near_count, part, variables), jnp.bfloat16),
            jax.ShapeDtypeStruct((far_count, part, variables), jnp.bfloat16),
            jax.ShapeDtypeStruct((8, LANES), jnp.int32),
        ),
        index,
        shards,
        scratch=(),
    )
    near = lax.all_to_all(near, "line", 0, 0)
    far = jnp.broadcast_to(far[None], (line_count,) + far.shape)
    near, far = lax.optimization_barrier((near, far))
    types = (own_type, sent_type)
    own, sent = call("forward0", first_kernel, types, table, side, near, scratch=())
    far = lax.all_to_all(far, "line", 0, 0)
    message_type = jax.ShapeDtypeStruct((2 * lines + TILE + 2 * variables, variables), jnp.bfloat16)

    def ahead(name, kind, level, own, sent, paired, across, blocks, is_first=False):
        count = len(paired), len(across), len(blocks)
        kernel = functools.partial(ahead_kernel, kind, level, count)
        args = (table, own, sent, *paired, *across, *blocks)
        message = call(name, kernel, message_type, *args)
        if is_first:
            across = [(i, ((i + 1) ^ 1) - 1) for i in range(1, blk_count - 1)]
            return lax.ppermute(message, "blk", across), sent
        return from_across(message, blk_count, line_count), sent

    def step(name, kind, level, own, paired, across, blocks, message=(), start=None, gives_now=True):
        extra = message if start is None else (*message, start)
        count = len(paired), len(across), len(blocks), bool(message), start is not None, gives_now
        kernel = functools.partial(level_kernel, kind, level, count)
        outs = (own_type,)
        if kind == LOWER or level > 0:
            outs += (sent_type,)
        if message:
            outs += (sent_type,) * (1 + gives_now)
        return call(name, kernel, outs, table, own, *paired, *across, *blocks, *extra)

    paired, across, ahead_of = (from_pair(sent, blk_count),), (), {}
    for level in range(1, LEVELS, 2):
        blocks = (near,) if level + 1 < LEVELS // 2 else (near, far)
        held = (near,) if level <= 3 else blocks
        ahead_args = own, sent, paired, across, held, level == 1
        message = ahead(f"ahead{level}", LOWER, level, *ahead_args)
        args = own, paired, across, blocks, message, None, level + 1 < LEVELS
        own, sent, ahead_of[level], *now = step(f"forward{level}", LOWER, level, *args)
        across += (*now, ahead_of[level])
        paired += (from_pair(sent, blk_count),)
        if level + 1 < LEVELS:
            args = own, paired, across, blocks
            own, sent = step(f"forward{level + 1}", LOWER, level + 1, *args)
            paired += (from_pair(sent, blk_count),)

    paired, across, blocks = paired[-1:], across[-1:], (near, far)
    for level in range(LEVELS - 2, -1, -2):
        own, *sent = step(f"backward{level}", UPPER, level, own, paired, across, blocks)
        if level == 0:
            break
        paired += (from_pair(sent[0], blk_count),)
        ahead_args = own, sent[0], paired, across, blocks
        message = ahead(f"behind{level - 1}", UPPER, level - 1, *ahead_args)
        args = own, paired, across, blocks, message, ahead_of[level - 1]
        own, sent, following, now = step(f"backward{level - 1}", UPPER, level - 1, *args)
        across += (now, following)
        paired += (from_pair(sent, blk_count),)
    return own


def solution(mesh):
    in_specs = (
        P("blk", "line", None),
        P("blk", "line", None),
        P("blk", None, "line", None),
        P("blk", None, "line", None),
        P("blk"),
        P("blk", None),
        P("blk", None),
    )
    out_specs = P("blk", "line", None)
    return jax.shard_map(local, mesh=mesh, in_specs=in_specs, out_specs=out_specs, check_vma=False)
```

```python
import functools

import jax
import jax.numpy as jnp
from jax import lax
from jax.experimental import pallas as pl
from jax.experimental.pallas import tpu as pltpu
from jax.sharding import PartitionSpec as P

LEVELS = 6
MOST_LEVEL = 3
LINKS = 3
NEAR_ROWS = 7
TILE = 16
LANES = 128
SPOT, ROW, FEW = 6, 4, 2
LOWER, UPPER, KEY = 0, 1, 2

VMEM = pl.BlockSpec(memory_space=pltpu.VMEM)


def from_pair(value, count):
    pairs = [[i, i + 1] for i in range(0, count, 2)]
    return lax.all_gather(value, "blk", axis=0, axis_index_groups=pairs)


def from_across(value, blk_count, line_count):
    groups = []
    for line in range(line_count):
        for blk in range(1, blk_count - 1, 2):
            groups.append([blk * line_count + line, (blk + 1) * line_count + line])
    for blk in (0, blk_count - 1):
        for line in range(0, line_count, 2):
            groups.append([blk * line_count + line, blk * line_count + line + 1])
    return lax.all_gather(value, ("blk", "line"), axis=0, axis_index_groups=groups)


def first_block(place):
    return MOST_LEVEL + (1 + LINKS) * place


def prepare_kernel(rows, index_ref, shards_ref, near_ref, far_ref, table_ref):
    me = lax.axis_index("blk")
    paired_side = 1 - 2 * lax.rem(me, 2)

    across_of = lax.broadcasted_iota(jnp.int32, (TILE, LANES), 1)
    down_of = lax.broadcasted_iota(jnp.int32, (TILE, LANES), 0)
    index = index_ref[...]
    level = jnp.broadcast_to(jnp.where(across_of[:1] < rows, index[:1], LEVELS), (TILE, LANES))
    level_down = jnp.sum(jnp.where(across_of == down_of, level, 0), axis=1, keepdims=True)
    is_row = down_of < rows
    is_less = (level_down < level) & is_row
    is_same = (level_down == level) & (down_of < across_of) & is_row
    in_level = jnp.sum(is_same.astype(jnp.int32), axis=0, keepdims=True)
    place_of = jnp.sum(is_less.astype(jnp.int32), axis=0, keepdims=True) + in_level
    number = across_of[:1]
    zeros = jnp.sum(((level == 0) & (down_of == 0)).astype(jnp.int32))

    def code(links):
        rel = links - me * rows
        side = (rel >= rows).astype(jnp.int32) - (rel < 0).astype(jnp.int32)
        there = rel - side * rows + jnp.where(side == paired_side, rows, 2 * rows)
        spot = jnp.clip(jnp.where(side == 0, rel, there), 0, 3 * rows - 1)
        packed = (number << (LINKS * SPOT)) | (place_of << (LINKS * SPOT + ROW))
        packed = packed | ((zeros | (1 << FEW)) << (LINKS * SPOT + 2 * ROW))
        for k in range(LINKS):
            packed = packed | (spot[k : k + 1] << (k * SPOT))
        return packed

    key = level[:1] * (MOST_LEVEL + 1) + in_level
    codes = [code(index[1 : 1 + LINKS]), code(index[1 + LINKS : 1 + 2 * LINKS]), key]
    table_ref[...] = jnp.concatenate(codes + [jnp.zeros_like(key)] * 5, axis=0)

    is_number = number < rows

    def row_at(place):
        return jnp.sum(jnp.where((place_of == place) & is_number, number, 0))

    def spread(block, part):
        for device in range(near_ref.shape[0]):
            near_ref[device, block] = part

    for place in range(MOST_LEVEL):
        spread(place, shards_ref[row_at(place), 0])
    for place in range(rows - 1):
        row = row_at(zeros + place)
        for k in range(1 + LINKS):
            if place < NEAR_ROWS:
                spread(first_block(place) + k, shards_ref[row, k])
            else:
                far_ref[first_block(place) - first_block(NEAR_ROWS) + k] = shards_ref[row, k]
    upper = first_block(rows - 1) - first_block(NEAR_ROWS)
    for place in range(rows - 1):
        row = row_at(place)
        for k in range(LINKS):
            far_ref[upper + LINKS * place + k] = shards_ref[row, 1 + LINKS + k]


def times(x, block):
    return lax.dot_general(x, block, (((1,), (1,)), ((), ())), preferred_element_type=jnp.float32)


def block_at(gathered_ref, index):
    count, _, part, variables = gathered_ref.shape
    return gathered_ref[:, index].reshape(count * part, variables)


def block_of(near_ref, far_ref, index):
    near = near_ref.shape[1]
    if far_ref is None:
        return block_at(near_ref, index)
    far_block = block_at(far_ref, jnp.maximum(index - near, 0))
    return jnp.where(index < near, block_at(near_ref, jnp.minimum(index, near - 1)), far_block)


def slots_of(table_ref, level, kind, count=MOST_LEVEL):
    table = table_ref[...]
    found, slots = [], []
    for slot in range(count):
        is_it = table[KEY : KEY + 1] == level * (MOST_LEVEL + 1) + slot
        code = jnp.sum(jnp.where(is_it, table[kind : kind + 1], 0))
        code = code if slot == 0 else jnp.where(code == 0, found[0], code)
        found.append(code)
        spots = [(code >> (k * SPOT)) & ((1 << SPOT) - 1) for k in range(LINKS)]
        row = (code >> (LINKS * SPOT)) & ((1 << ROW) - 1)
        place = (code >> (LINKS * SPOT + ROW)) & ((1 << ROW) - 1)
        zeros = (code >> (LINKS * SPOT + 2 * ROW)) & ((1 << FEW) - 1)
        inverse_at = first_block(place - zeros) if level else place
        slots.append((row, inverse_at, LINKS * place, spots))
    return slots


def joined(parts):
    return jnp.concatenate(parts, axis=1)


def put_message(ref, value, number):
    lines, variables = value.shape
    ref[pl.ds(0, lines)] = value
    number = jnp.full((TILE, variables), number, jnp.int32).astype(jnp.float32)
    ref[pl.ds(lines, TILE)] = number.astype(jnp.bfloat16)


def number_in(ref, lines):
    return jnp.max(ref[pl.ds(lines, TILE)].astype(jnp.float32)).astype(jnp.int32)


def lay_out(pool_ref, own_ref, paired_refs, across_refs):
    rows, lines = own_ref.shape[0], own_ref.shape[1]
    pool_ref[pl.ds(0, rows)] = own_ref[...]
    other = 1 - lax.rem(lax.axis_index("blk"), 2)
    for ref in paired_refs:
        message = ref.at[other] if len(ref.shape) == 3 else ref
        pool_ref[rows + number_in(message, lines)] = message[pl.ds(0, lines)]
    numbers = []
    for ref in across_refs:
        numbers.append(number_in(ref, lines))
        pool_ref[2 * rows + numbers[-1]] = ref[pl.ds(0, lines)]
    return numbers


def blocks_for(kind, rows, near_ref, far_ref, inverse_at, upper_at):
    if kind == LOWER:
        return [block_of(near_ref, far_ref, inverse_at + 1 + k) for k in range(LINKS)]
    upper_at += first_block(rows - 1) - near_ref.shape[1]
    return [block_at(far_ref, upper_at + k) for k in range(LINKS)]


def solve(kind, start, pulled, inverse):
    if kind == LOWER:
        reduced = (start.astype(jnp.float32) - pulled).astype(jnp.bfloat16)
        return times(reduced, inverse).astype(jnp.bfloat16)
    taken = times(pulled.astype(jnp.bfloat16), inverse)
    return (start.astype(jnp.float32) - taken).astype(jnp.bfloat16)


def first_kernel(table_ref, side_ref, near_ref, own_ref, sent_ref):
    own_ref[...] = side_ref[...]
    for slot, (row, inverse_at, _, _) in enumerate(slots_of(table_ref, 0, LOWER)):
        solved = times(side_ref[row], block_at(near_ref, inverse_at)).astype(jnp.bfloat16)
        own_ref[row] = solved
        if slot == 0:
            put_message(sent_ref, solved, row)


def ahead_kernel(kind, level, count, *refs):
    count_paired, count_across, count_blocks = count
    table_ref, own_ref, sent_ref = refs[:3]
    refs = refs[3:]
    paired_refs, refs = refs[:count_paired], refs[count_paired:]
    across_refs, refs = refs[:count_across], refs[count_across:]
    near_ref, far_ref = refs[0], refs[1] if count_blocks == 2 else None
    out_ref, pool_ref = refs[-2:]
    rows, lines = own_ref.shape[0], own_ref.shape[1]
    row, inverse_at, upper_at, spots = slots_of(table_ref, level, kind, 1)[0]
    numbers = lay_out(pool_ref, own_ref, paired_refs, across_refs)
    blocks = blocks_for(kind, rows, near_ref, far_ref, inverse_at, upper_at)
    sources, lacking = [], jnp.zeros(blocks[0].shape, jnp.float32)
    for spot, block in zip(spots, blocks):
        is_lacking = spot >= 2 * rows
        for number in numbers:
            is_lacking &= spot != 2 * rows + number
        source = pool_ref[spot]
        sources.append(jnp.where(is_lacking, jnp.zeros_like(source), source))
        lacking += jnp.where(is_lacking, block, jnp.zeros_like(block)).astype(jnp.float32)
    known = times(joined(sources), joined(blocks))
    if kind == LOWER:
        known = own_ref[row].astype(jnp.float32) - known
    variables = known.shape[1]
    number = number_in(sent_ref, lines) + TILE * row
    out_ref[pl.ds(0, lines)] = sent_ref[pl.ds(0, lines)]
    tile = jnp.full((TILE, variables), number, jnp.int32).astype(jnp.float32)
    out_ref[pl.ds(lines, TILE)] = tile.astype(jnp.bfloat16)
    out_ref[pl.ds(lines + TILE, lines)] = known.astype(jnp.bfloat16)
    out_ref[pl.ds(2 * lines + TILE, variables)] = lacking.astype(jnp.bfloat16)
    inverse = block_of(near_ref, far_ref, inverse_at)
    out_ref[pl.ds(2 * lines + TILE + variables, variables)] = inverse


def level_kernel(kind, level, count, *refs):
    count_paired, count_across, count_blocks, has_message, has_start, gives_now, gives_pair = count
    table_ref, old_ref = refs[:2]
    refs = refs[2:]
    paired_refs, refs = refs[:count_paired], refs[count_paired:]
    across_refs, refs = refs[:count_across], refs[count_across:]
    near_ref, far_ref = refs[0], refs[1] if count_blocks == 2 else None
    refs = refs[count_blocks:]
    pool_ref, refs = refs[-1], refs[:-1]
    pair_ref, refs = (refs[-1], refs[:-1]) if gives_pair else (None, refs)
    rows, lines, variables = old_ref.shape
    slots = slots_of(table_ref, level, kind)
    lay_out(pool_ref, old_ref, paired_refs, across_refs)
    if has_message:
        message, mine_ref, refs = refs[0], refs[1], refs[2:]
        start_ref, refs = (refs[0], refs[1:]) if has_start else (None, refs)
        own_ref, sent_ref, next_ref = refs[:3]
        if len(message.shape) == 3:
            message = message.at[lax.rem(lax.axis_index("blk"), 2)]
        numbers = number_in(message, lines)
        number_next = numbers // TILE
        number_now = numbers - TILE * number_next
        across_now = message[pl.ds(0, lines)]
        pool_ref[2 * rows + number_now] = across_now
        if gives_now:
            put_message(refs[3], across_now, number_now)
        known = message[pl.ds(lines + TILE, lines)]
        lacking = message[pl.ds(2 * lines + TILE, variables)]
        inverse = message[pl.ds(2 * lines + TILE + variables, variables)]
        added = times(mine_ref[pl.ds(0, lines)], lacking)
        if kind == LOWER:
            across_next = solve(kind, known, added, inverse)
        else:
            start = start_ref[pl.ds(0, lines)]
            across_next = solve(kind, start, known.astype(jnp.float32) + added, inverse)
        put_message(next_ref, across_next, number_next)
    else:
        own_ref, sent_ref = refs if len(refs) == 2 else (refs[0], None)
    if gives_pair:
        pair = paired_refs[-1].at[1 - lax.rem(lax.axis_index("blk"), 2)]
        pair_ref[...] = pair[...]
    own_ref[...] = old_ref[...]
    solved_all = []
    for row, inverse_at, upper_at, spots in slots:
        blocks = blocks_for(kind, rows, near_ref, far_ref, inverse_at, upper_at)
        pulled = times(joined([pool_ref[spot] for spot in spots]), joined(blocks))
        inverse = block_of(near_ref, far_ref, inverse_at)
        solved_all.append((row, solve(kind, old_ref[row], pulled, inverse)))
    if sent_ref is not None:
        put_message(sent_ref, solved_all[0][1], solved_all[0][0])
    for row, solved in solved_all:
        own_ref[row] = solved


def local(
    right_side, diagonal_inverse, lower_blocks, upper_blocks, row_level, lower_links, upper_links
):
    rows, lines, variables = right_side.shape
    part = diagonal_inverse.shape[1]
    blk_count, line_count = lax.axis_size("blk"), lax.axis_size("line")
    own_type = jax.ShapeDtypeStruct((rows, lines, variables), jnp.bfloat16)
    sent_type = jax.ShapeDtypeStruct((lines + TILE, variables), jnp.bfloat16)
    pool = pltpu.VMEM((3 * rows, lines, variables), jnp.bfloat16)

    def call(name, kernel, out_shape, *args, scratch=(pool,)):
        return pl.pallas_call(
            kernel,
            out_shape=out_shape,
            in_specs=[VMEM] * len(args),
            out_specs=jax.tree.map(lambda _: VMEM, out_shape),
            scratch_shapes=scratch,
            compiler_params=pltpu.CompilerParams(vmem_limit_bytes=32 * 1024 * 1024),
            name=name,
        )(*args)

    side = right_side
    index = jnp.concatenate([row_level[None], lower_links.T, upper_links.T], axis=0)
    index = jnp.pad(index, ((0, 8 - index.shape[0]), (0, LANES - rows)))
    shards = jnp.concatenate([diagonal_inverse[:, None], lower_blocks, upper_blocks], axis=1)
    near_count = first_block(NEAR_ROWS)
    far_count = first_block(rows - 1) - near_count + LINKS * (rows - 1)
    near, far, table = call(
        "prepare",
        functools.partial(prepare_kernel, rows),
        (
            jax.ShapeDtypeStruct((line_count, near_count, part, variables), jnp.bfloat16),
            jax.ShapeDtypeStruct((far_count, part, variables), jnp.bfloat16),
            jax.ShapeDtypeStruct((8, LANES), jnp.int32),
        ),
        index,
        shards,
        scratch=(),
    )
    near = lax.all_to_all(near, "line", 0, 0)
    far = jnp.broadcast_to(far[None], (line_count,) + far.shape)
    near, far = lax.optimization_barrier((near, far))
    types = (own_type, sent_type)
    own, sent = call("forward0", first_kernel, types, table, side, near, scratch=())
    far = lax.all_to_all(far, "line", 0, 0)
    message_type = jax.ShapeDtypeStruct((2 * lines + TILE + 2 * variables, variables), jnp.bfloat16)

    def ahead(name, kind, level, own, sent, paired, across, blocks, is_first=False):
        count = len(paired), len(across), len(blocks)
        kernel = functools.partial(ahead_kernel, kind, level, count)
        args = (table, own, sent, *paired, *across, *blocks)
        message = call(name, kernel, message_type, *args)
        if is_first:
            across = [(i, ((i + 1) ^ 1) - 1) for i in range(1, blk_count - 1)]
            return lax.ppermute(message, "blk", across), sent
        return from_across(message, blk_count, line_count), sent

    def step(name, kind, level, own, paired, across, blocks, message=(), start=None, gives_now=True):
        extra = message if start is None else (*message, start)
        gives_pair = kind == LOWER and level <= 2
        count = len(paired), len(across), len(blocks), bool(message), start is not None, gives_now
        count += (gives_pair,)
        kernel = functools.partial(level_kernel, kind, level, count)
        outs = (own_type,)
        if kind == LOWER or level > 0:
            outs += (sent_type,)
        if message:
            outs += (sent_type,) * (1 + gives_now)
        outs += (sent_type,) * gives_pair
        return call(name, kernel, outs, table, own, *paired, *across, *blocks, *extra)

    paired, across, ahead_of = (from_pair(sent, blk_count),), (), {}
    for level in range(1, LEVELS, 2):
        blocks = (near,) if level + 1 < LEVELS // 2 else (near, far)
        held = (near,) if level <= 3 else blocks
        ahead_args = own, sent, paired, across, held, level == 1
        message = ahead(f"ahead{level}", LOWER, level, *ahead_args)
        args = own, paired, across, blocks, message, None, level + 1 < LEVELS
        own, sent, ahead_of[level], *now = step(f"forward{level}", LOWER, level, *args)
        if level == 1:
            now, paired = now[:1], tuple(now[1:])
        across += (*now, ahead_of[level])
        paired += (from_pair(sent, blk_count),)
        if level + 1 < LEVELS:
            args = own, paired, across, blocks
            own, sent, *kept = step(f"forward{level + 1}", LOWER, level + 1, *args)
            paired = paired[: len(paired) - len(kept)] + tuple(kept)
            paired += (from_pair(sent, blk_count),)

    paired, across, blocks = paired[-1:], across[-1:], (near, far)
    for level in range(LEVELS - 2, -1, -2):
        own, *sent = step(f"backward{level}", UPPER, level, own, paired, across, blocks)
        if level == 0:
            break
        paired += (from_pair(sent[0], blk_count),)
        ahead_args = own, sent[0], paired, across, blocks
        message = ahead(f"behind{level - 1}", UPPER, level - 1, *ahead_args)
        args = own, paired, across, blocks, message, ahead_of[level - 1]
        own, sent, following, now = step(f"backward{level - 1}", UPPER, level - 1, *args)
        across += (now, following)
        paired += (from_pair(sent, blk_count),)
    return own


def solution(mesh):
    in_specs = (
        P("blk", "line", None),
        P("blk", "line", None),
        P("blk", None, "line", None),
        P("blk", None, "line", None),
        P("blk"),
        P("blk", None),
        P("blk", None),
    )
    out_specs = P("blk", "line", None)
    return jax.shard_map(local, mesh=mesh, in_specs=in_specs, out_specs=out_specs, check_vma=False)
```

```python
import collections
import functools

import jax
import jax.numpy as jnp
from jax import lax
from jax.experimental import pallas as pl
from jax.experimental.pallas import tpu as pltpu
from jax.sharding import PartitionSpec as P

LEVELS = 6
MOST_LEVEL = 3
LINKS = 3
NEAR_ROWS = 7
TILE = 16
LANES = 128
SPOT, ROW, FEW = 6, 4, 2
LOWER, UPPER, KEY = 0, 1, 2
PAIR, ACROSS = 1, 2

VMEM = pl.BlockSpec(memory_space=pltpu.VMEM)


def from_pair(value, count):
    pairs = [[i, i + 1] for i in range(0, count, 2)]
    return lax.all_gather(value, "blk", axis=0, axis_index_groups=pairs)


def from_across(value, blk_count, line_count):
    groups = []
    for line in range(line_count):
        for blk in range(1, blk_count - 1, 2):
            groups.append([blk * line_count + line, (blk + 1) * line_count + line])
    for blk in (0, blk_count - 1):
        for line in range(0, line_count, 2):
            groups.append([blk * line_count + line, blk * line_count + line + 1])
    return lax.all_gather(value, ("blk", "line"), axis=0, axis_index_groups=groups)


def first_block(place):
    return MOST_LEVEL + (1 + LINKS) * place


def prepare_kernel(rows, index_ref, shards_ref, near_ref, far_ref, table_ref):
    me = lax.axis_index("blk")
    paired_side = 1 - 2 * lax.rem(me, 2)

    across_of = lax.broadcasted_iota(jnp.int32, (TILE, LANES), 1)
    down_of = lax.broadcasted_iota(jnp.int32, (TILE, LANES), 0)
    index = index_ref[...]
    level = jnp.broadcast_to(jnp.where(across_of[:1] < rows, index[:1], LEVELS), (TILE, LANES))
    level_down = jnp.sum(jnp.where(across_of == down_of, level, 0), axis=1, keepdims=True)
    is_row = down_of < rows
    is_less = (level_down < level) & is_row
    is_same = (level_down == level) & (down_of < across_of) & is_row
    in_level = jnp.sum(is_same.astype(jnp.int32), axis=0, keepdims=True)
    place_of = jnp.sum(is_less.astype(jnp.int32), axis=0, keepdims=True) + in_level
    number = across_of[:1]
    zeros = jnp.sum(((level == 0) & (down_of == 0)).astype(jnp.int32))

    def code(links):
        rel = links - me * rows
        side = (rel >= rows).astype(jnp.int32) - (rel < 0).astype(jnp.int32)
        there = rel - side * rows + jnp.where(side == paired_side, rows, 2 * rows)
        spot = jnp.clip(jnp.where(side == 0, rel, there), 0, 3 * rows - 1)
        packed = (number << (LINKS * SPOT)) | (place_of << (LINKS * SPOT + ROW))
        packed = packed | ((zeros | (1 << FEW)) << (LINKS * SPOT + 2 * ROW))
        for k in range(LINKS):
            packed = packed | (spot[k : k + 1] << (k * SPOT))
        return packed

    key = level[:1] * (MOST_LEVEL + 1) + in_level
    codes = [code(index[1 : 1 + LINKS]), code(index[1 + LINKS : 1 + 2 * LINKS]), key]
    table_ref[...] = jnp.concatenate(codes + [jnp.zeros_like(key)] * 5, axis=0)

    is_number = number < rows

    def row_at(place):
        return jnp.sum(jnp.where((place_of == place) & is_number, number, 0))

    def spread(block, part):
        for device in range(near_ref.shape[0]):
            near_ref[device, block] = part

    for place in range(MOST_LEVEL):
        spread(place, shards_ref[row_at(place), 0])
    for place in range(rows - 1):
        row = row_at(zeros + place)
        for k in range(1 + LINKS):
            if place < NEAR_ROWS:
                spread(first_block(place) + k, shards_ref[row, k])
            else:
                far_ref[first_block(place) - first_block(NEAR_ROWS) + k] = shards_ref[row, k]
    upper = first_block(rows - 1) - first_block(NEAR_ROWS)
    for place in range(rows - 1):
        row = row_at(place)
        for k in range(LINKS):
            far_ref[upper + LINKS * place + k] = shards_ref[row, 1 + LINKS + k]


def times(x, block):
    return lax.dot_general(x, block, (((1,), (1,)), ((), ())), preferred_element_type=jnp.float32)


def block_at(gathered_ref, index):
    count, _, part, variables = gathered_ref.shape
    return gathered_ref[:, index].reshape(count * part, variables)


def block_of(near_ref, far_ref, index):
    near = near_ref.shape[1]
    if far_ref is None:
        return block_at(near_ref, index)
    far_block = block_at(far_ref, jnp.maximum(index - near, 0))
    return jnp.where(index < near, block_at(near_ref, jnp.minimum(index, near - 1)), far_block)


def slots_of(table_ref, level, kind, count=MOST_LEVEL):
    table = table_ref[...]
    found, slots = [], []
    for slot in range(count):
        is_it = table[KEY : KEY + 1] == level * (MOST_LEVEL + 1) + slot
        code = jnp.sum(jnp.where(is_it, table[kind : kind + 1], 0))
        code = code if slot == 0 else jnp.where(code == 0, found[0], code)
        found.append(code)
        spots = [(code >> (k * SPOT)) & ((1 << SPOT) - 1) for k in range(LINKS)]
        row = (code >> (LINKS * SPOT)) & ((1 << ROW) - 1)
        place = (code >> (LINKS * SPOT + ROW)) & ((1 << ROW) - 1)
        zeros = (code >> (LINKS * SPOT + 2 * ROW)) & ((1 << FEW) - 1)
        inverse_at = first_block(place - zeros) if level else place
        slots.append((row, inverse_at, LINKS * place, spots))
    return slots


def joined(parts):
    return jnp.concatenate(parts, axis=1)


def put_message(ref, value, number):
    lines, variables = value.shape
    ref[pl.ds(0, lines)] = value
    number = jnp.full((TILE, variables), number, jnp.int32).astype(jnp.float32)
    ref[pl.ds(lines, TILE)] = number.astype(jnp.bfloat16)


def number_in(ref, lines):
    return jnp.max(ref[pl.ds(lines, TILE)].astype(jnp.float32)).astype(jnp.int32)


def is_second(side):
    odd = lax.rem(lax.axis_index("blk"), 2)
    return odd if side == PAIR else 1 - odd


def lay_out(pool_ref, own_ref, known):
    rows, lines = own_ref.shape[0], own_ref.shape[1]
    pool_ref[pl.ds(0, rows)] = own_ref[...]
    numbers = {}
    for side, refs in known.items():
        numbers[side] = []
        for ref in refs:
            row_ref = ref.at[1 - is_second(side)] if len(ref.shape) == 3 else ref
            numbers[side].append(number_in(row_ref, lines))
            pool_ref[side * rows + numbers[side][-1]] = row_ref[pl.ds(0, lines)]
    return numbers


def blocks_for(kind, rows, near_ref, far_ref, inverse_at, upper_at):
    if kind == LOWER:
        return [block_of(near_ref, far_ref, inverse_at + 1 + k) for k in range(LINKS)]
    upper_at += first_block(rows - 1) - near_ref.shape[1]
    return [block_at(far_ref, upper_at + k) for k in range(LINKS)]


def solve(kind, start, pulled, inverse):
    if kind == LOWER:
        reduced = (start.astype(jnp.float32) - pulled).astype(jnp.bfloat16)
        return times(reduced, inverse).astype(jnp.bfloat16)
    taken = times(pulled.astype(jnp.bfloat16), inverse)
    return (start.astype(jnp.float32) - taken).astype(jnp.bfloat16)


def first_kernel(table_ref, side_ref, near_ref, own_ref, sent_ref):
    own_ref[...] = side_ref[...]
    for slot, (row, inverse_at, _, _) in enumerate(slots_of(table_ref, 0, LOWER)):
        solved = times(side_ref[row], block_at(near_ref, inverse_at)).astype(jnp.bfloat16)
        own_ref[row] = solved
        if slot == 0:
            put_message(sent_ref, solved, row)


Plan = collections.namedtuple(
    "Plan",
    [
        "kind",
        "level",
        "known",
        "blocks",
        "side_in",
        "start",
        "gives_now",
        "keeps",
        "side_out",
        "next_kind",
        "next_level",
    ],
)


def put_ahead(plan, out_ref, first, table_ref, own_ref, pool_ref, numbers, near_ref, far_ref):
    rows, lines, variables = own_ref.shape
    kind, side = plan.next_kind, plan.side_out
    row, inverse_at, upper_at, spots = slots_of(table_ref, plan.next_level, kind, 1)[0]
    blocks = blocks_for(kind, rows, near_ref, far_ref, inverse_at, upper_at)
    sources, lacking = [], jnp.zeros(blocks[0].shape, jnp.float32)
    for spot, block in zip(spots, blocks):
        is_lacking = (spot >= side * rows) & (spot < (side + 1) * rows)
        for number in numbers[side]:
            is_lacking &= spot != side * rows + number
        source = pool_ref[spot]
        sources.append(jnp.where(is_lacking, jnp.zeros_like(source), source))
        lacking += jnp.where(is_lacking, block, jnp.zeros_like(block)).astype(jnp.float32)
    known = times(joined(sources), joined(blocks))
    if kind == LOWER:
        known = pool_ref[row].astype(jnp.float32) - known
    put_message(out_ref, first[1], first[0] + TILE * row)
    out_ref[pl.ds(lines + TILE, lines)] = known.astype(jnp.bfloat16)
    out_ref[pl.ds(2 * lines + TILE, variables)] = lacking.astype(jnp.bfloat16)
    if kind == LOWER or side == PAIR:
        inverse = block_of(near_ref, far_ref, inverse_at)
        out_ref[pl.ds(2 * lines + TILE + variables, variables)] = inverse


def level_kernel(plan, *refs):
    refs = list(refs)
    kind, level, side_in = plan.kind, plan.level, plan.side_in

    def take(count):
        return [refs.pop(0) for _ in range(count)]

    table_ref, old_ref = take(2)
    known = {side: take(count) for side, count in zip((PAIR, ACROSS), plan.known)}
    near_ref, far_ref = (take(plan.blocks) + [None])[:2]
    (message_ref,) = take(1) if side_in else [None]
    (start_ref,) = take(1) if plan.start else [None]
    (inverse_ref,) = take(1) if kind == UPPER and side_in == ACROSS else [None]
    (own_ref,) = take(1) if level is not None else [None]
    (out_ref,) = take(1) if plan.side_out else [None]
    (next_ref,) = take(1) if side_in else [None]
    (now_ref,) = take(1) if plan.gives_now else [None]
    (kept_ref,) = take(1) if plan.keeps else [None]
    (pool_ref,) = refs
    rows, lines, variables = old_ref.shape

    numbers = lay_out(pool_ref, old_ref, known)
    if side_in:
        message = message_ref
        if len(message_ref.shape) == 3:
            message = message_ref.at[1 - is_second(side_in)]
        both = number_in(message, lines)
        number_next = both // TILE
        number_now = both - TILE * number_next
        row_now = message[pl.ds(0, lines)]
        before = slots_of(table_ref, level - 1 if kind == LOWER else level + 1, kind, 1)[0][0]
        start = message[pl.ds(lines + TILE, lines)]
        added = times(old_ref[before], message[pl.ds(2 * lines + TILE, variables)])
        if inverse_ref is None:
            inverse = message[pl.ds(2 * lines + TILE + variables, variables)]
        else:
            inverse = inverse_ref[...]
        if plan.keeps:
            kept_ref[...] = inverse
        if kind == UPPER:
            added += start.astype(jnp.float32)
            start = start_ref[pl.ds(0, lines)]
        row_next = solve(kind, start, added, inverse)
        pool_ref[side_in * rows + number_now] = row_now
        put_message(next_ref, row_next, number_next)
        if plan.gives_now:
            put_message(now_ref, row_now, number_now)

    if level is None:
        row = slots_of(table_ref, 0, LOWER, 1)[0][0]
        solved_all = [(row, old_ref[row])]
    else:
        solved_all = []
        for row, inverse_at, upper_at, spots in slots_of(table_ref, level, kind):
            blocks = blocks_for(kind, rows, near_ref, far_ref, inverse_at, upper_at)
            pulled = times(joined([pool_ref[spot] for spot in spots]), joined(blocks))
            inverse = block_of(near_ref, far_ref, inverse_at)
            solved_all.append((row, solve(kind, old_ref[row], pulled, inverse)))
        own_ref[...] = old_ref[...]
        for row, solved in solved_all:
            own_ref[row] = solved

    if plan.next_kind is not None:
        if side_in:
            pool_ref[side_in * rows + number_next] = row_next
            numbers[side_in] += [number_now, number_next]
        if level is not None:
            for row, solved in solved_all:
                pool_ref[row] = solved
        put_ahead(
            plan, out_ref, solved_all[0], table_ref, old_ref, pool_ref, numbers, near_ref, far_ref
        )
    elif plan.side_out:
        put_message(out_ref, solved_all[0][1], solved_all[0][0])


def local(
    right_side, diagonal_inverse, lower_blocks, upper_blocks, row_level, lower_links, upper_links
):
    rows, lines, variables = right_side.shape
    part = diagonal_inverse.shape[1]
    blk_count, line_count = lax.axis_size("blk"), lax.axis_size("line")
    own_type = jax.ShapeDtypeStruct((rows, lines, variables), jnp.bfloat16)
    sent_type = jax.ShapeDtypeStruct((lines + TILE, variables), jnp.bfloat16)
    pool = pltpu.VMEM((3 * rows, lines, variables), jnp.bfloat16)

    def call(name, kernel, out_shape, *args, scratch=(pool,)):
        return pl.pallas_call(
            kernel,
            out_shape=out_shape,
            in_specs=[VMEM] * len(args),
            out_specs=jax.tree.map(lambda _: VMEM, out_shape),
            scratch_shapes=scratch,
            compiler_params=pltpu.CompilerParams(vmem_limit_bytes=32 * 1024 * 1024),
            name=name,
        )(*args)

    side = right_side
    index = jnp.concatenate([row_level[None], lower_links.T, upper_links.T], axis=0)
    index = jnp.pad(index, ((0, 8 - index.shape[0]), (0, LANES - rows)))
    shards = jnp.concatenate([diagonal_inverse[:, None], lower_blocks, upper_blocks], axis=1)
    near_count = first_block(NEAR_ROWS)
    far_count = first_block(rows - 1) - near_count + LINKS * (rows - 1)
    near, far, table = call(
        "prepare",
        functools.partial(prepare_kernel, rows),
        (
            jax.ShapeDtypeStruct((line_count, near_count, part, variables), jnp.bfloat16),
            jax.ShapeDtypeStruct((far_count, part, variables), jnp.bfloat16),
            jax.ShapeDtypeStruct((8, LANES), jnp.int32),
        ),
        index,
        shards,
        scratch=(),
    )
    near = lax.all_to_all(near, "line", 0, 0)
    far = jnp.broadcast_to(far[None], (line_count,) + far.shape)
    near, far = lax.optimization_barrier((near, far))
    types = (own_type, sent_type)
    own, sent = call("forward0", first_kernel, types, table, side, near, scratch=())
    far = lax.all_to_all(far, "line", 0, 0)
    block_type = jax.ShapeDtypeStruct((variables, variables), jnp.bfloat16)

    def step(name, kind, level, own, known, blocks, next_kind=None, next_level=None, **options):
        message, start = options.get("message"), options.get("start")
        side_in, side_out = options.get("side_in", 0), options.get("side_out", 0)
        gives_now = options.get("gives_now", True) and bool(side_in)
        counts = len(known[PAIR]), len(known[ACROSS])
        keeps, inverse = options.get("keeps", False), options.get("inverse")
        plan = Plan(
            *(kind, level, counts, len(blocks), side_in, start is not None, gives_now, keeps),
            *(side_out, next_kind, next_level),
        )
        sent_blocks = 1 if next_kind == UPPER and side_out == ACROSS else 2
        message_rows = 2 * lines + TILE + sent_blocks * variables
        message_type = jax.ShapeDtypeStruct((message_rows, variables), jnp.bfloat16)
        outs = () if level is None else (own_type,)
        if side_out:
            outs += (sent_type if next_kind is None else message_type,)
        outs += (sent_type,) * (bool(side_in) + gives_now) + (block_type,) * keeps
        args = (table, own, *known[PAIR], *known[ACROSS], *blocks)
        args += tuple(x for x in (message, start, inverse) if x is not None)
        return call(name, functools.partial(level_kernel, plan), outs, *args)

    def exchange(side, value):
        if side == PAIR:
            return from_pair(value, blk_count)
        return from_across(value, blk_count, line_count)

    known = {PAIR: (from_pair(sent, blk_count),), ACROSS: ()}
    options = {"side_out": ACROSS}
    (out,) = step("ahead", LOWER, None, own, known, (near,), LOWER, 1, **options)
    across = [(i, ((i + 1) ^ 1) - 1) for i in range(1, blk_count - 1)]
    message = lax.ppermute(out, "blk", across)
    ahead, kept = {}, {}
    for level in range(1, LEVELS):
        side_in, side_out = (ACROSS, PAIR) if level % 2 else (PAIR, ACROSS)
        blocks = (near,) if level < LEVELS // 2 else (near, far)
        is_last = level + 1 == LEVELS
        following = (UPPER, LEVELS - 2) if is_last else (LOWER, level + 1)
        options = {"message": message, "side_in": side_in, "side_out": side_out}
        options["gives_now"] = not is_last
        options["keeps"] = side_in == ACROSS and not is_last
        args = own, known, blocks, *following
        own, out, ahead[level], *now = step(f"forward{level}", LOWER, level, *args, **options)
        if options["keeps"]:
            kept[level] = now.pop()
        known[side_in] += (*now, ahead[level])
        message = exchange(side_out, out)

    known = {PAIR: (), ACROSS: (ahead[LEVELS - 1],)}
    blocks = near, far
    for level in range(LEVELS - 2, 0, -1):
        side_in, side_out = (ACROSS, PAIR) if level % 2 else (PAIR, ACROSS)
        following = (UPPER, level - 1) if level > 1 else ()
        options = {"message": message, "side_in": side_in, "side_out": side_out}
        options["start"], options["inverse"] = ahead[level], kept.get(level)
        args = own, known, blocks, *following
        own, out, *rows_in = step(f"backward{level}", UPPER, level, *args, **options)
        known[side_in] += tuple(rows_in)
        message = exchange(side_out, out)
    known[PAIR] += (message,)
    return step("backward0", UPPER, 0, own, known, blocks)[0]


def solution(mesh):
    in_specs = (
        P("blk", "line", None),
        P("blk", "line", None),
        P("blk", None, "line", None),
        P("blk", None, "line", None),
        P("blk"),
        P("blk", None),
        P("blk", None),
    )
    out_specs = P("blk", "line", None)
    return jax.shard_map(local, mesh=mesh, in_specs=in_specs, out_specs=out_specs, check_vma=False)
```
